128 devices in a mesh: expert: 32 (over x, z, core), shard: 4 (over y).
Axes of the slice: x: 4, y: 4, z: 4, core: 2. Of those that a mesh axis runs over, the one named last changes fastest.
Arguments:
- tokens: bfloat16 [16384, 768], P('expert'), may hold values from -6 to 6
- qkv_weight: bfloat16 [3, 768, 768], P(None, None, 'shard'), may hold values from -0.21875 to 0.21875
- out_proj: bfloat16 [768, 768], P('shard'), may hold values from -0.875 to 0.875
- rel_bias: float32 [12, 32], P('shard'), may hold values from -6 to 6
- gains: float32 [2, 768], replicated, may hold values from 0.5 to 1.5
- router: bfloat16 [768, 32], replicated, may hold values from -0.109375 to 0.109375
- w_in: bfloat16 [32, 768, 3072], P('expert', None, 'shard'), may hold values from -0.21875 to 0.21875
- w_out: bfloat16 [32, 3072, 768], P('expert', 'shard'), may hold values from -7 to 7
- route: int32 [16384], P('expert'), may hold values from 0 to 31, as said below
- slot: int32 [16384], P('expert'), may hold values from 0 to 23, as said below
- buckets: int32 [1023], replicated, may hold values from 0 to 31, as said below
- cotangent: bfloat16 [16384, 768], P('expert'), may hold values from -6 to 6
Outputs:
- result: bfloat16 [16384, 768], P('expert')
- grad_tokens: bfloat16 [16384, 768], P('expert')
- grad_qkv: float32 [3, 768, 768], P(None, None, 'shard')
- grad_out_proj: float32 [768, 768], P('shard')
- grad_bias: float32 [12, 32], P('shard')
- grad_gains: float32 [2, 768], replicated
- grad_router: float32 [768, 32], replicated
- grad_w_in: float32 [32, 768, 3072], P('expert', None, 'shard')
- grad_w_out: float32 [32, 3072, 768], P('expert', 'shard')
The draws below stay inside these ranges and needn't reach their ends.
Inputs may be any that keep to these rules, and one draw needn't show every extreme that they name: Within each aligned block of 512 rows (one sequence) no two rows share both route and slot, and in every block some expert has all 24 slots taken. `slot`: paired with route as stated there. Entry j - i + 511 is the bucket of offset j - i: 0 for offset 0, buckets 0 to 15 for offsets of at most 0 and the rest for positive ones, never falling with the size of the offset within one sign.
All inputs are finite; a program needn't handle non-finite values.
Results may differ from the reference program's by a relative error of at most 0.03.
Values may be sent and summed in bfloat16 or wider, within the bound.
No kernel may reach another device: no remote copies, remote signals or barrier semaphores. Data moves between devices by JAX's collectives and lax.ppermute only.
A program may use at most 128 MiB of HBM per device.

```python
import jax
import jax.numpy as jnp
from jax import lax

D = 768
HEADS = 12
HEAD_DIM = 64
FF = 3072
BUCKETS = 32
LEN = 512
EXPERTS = 32
CAP = 24
TOKENS = 16384
N_EXPERT = 32


def route_plan(key):
    pool_size = EXPERTS * CAP

    def one_group(group_key):
        key_one, key_two, key_three = jax.random.split(group_key, 3)
        order = jax.random.permutation(key_one, pool_size)
        ranking = jnp.zeros(pool_size, jnp.int32).at[order].set(jnp.arange(pool_size, dtype=jnp.int32))
        full_expert = jax.random.randint(key_two, (), 0, EXPERTS)
        owner = jnp.arange(pool_size, dtype=jnp.int32) // CAP
        priority = jnp.where(owner == full_expert, ranking - pool_size, ranking)
        picked = jnp.argsort(priority, stable=True)[:LEN]
        shuffle = jax.random.permutation(key_three, LEN)
        picked = picked[shuffle].astype(jnp.int32)
        return (picked // CAP, picked % CAP)
    group_keys = jax.random.split(key, TOKENS // LEN)
    experts_of, slots_of = jax.vmap(one_group)(group_keys)
    return (experts_of.reshape(-1).astype(jnp.int32), slots_of.reshape(-1).astype(jnp.int32))


def draw_route(key, part):
    plan = route_plan(key)
    return plan[0]


def draw_slot(key, part):
    plan = route_plan(key)
    return plan[1]


def draw_buckets(key, part):
    key = jax.random.fold_in(key, 3)
    half_count = BUCKETS // 2
    bounds = jnp.sort(jax.random.permutation(key, LEN - 1)[:half_count - 1] + 1)
    offsets = jnp.arange(2 * LEN - 1, dtype=jnp.int32) - (LEN - 1)
    magnitude = jnp.abs(offsets)
    level = jnp.sum((bounds[None, :] <= magnitude[:, None]).astype(jnp.int32), axis=1)
    return (level + half_count * (offsets > 0).astype(jnp.int32)).astype(jnp.int32)


def steps_of(own_key, extent, pieces, least, top_value):
    def one(axis_at, blocks):
        draws = jax.random.uniform(jax.random.fold_in(jax.random.fold_in(own_key, 6), axis_at), (blocks,), jnp.float32, least / len(pieces), top_value / len(pieces))
        return jnp.repeat(jnp.exp(draws), extent[axis_at] // blocks).reshape((-1,) + (1,) * (len(extent) - axis_at - 1))

    gain = one(*pieces[0])
    for cut in pieces[1:]:
        gain = gain * one(*cut)
    return gain


def normal_values(stream_key, extent, spread, limit, cuts=(), kind=jnp.bfloat16):
    array = jax.random.normal(stream_key, extent, jnp.float32) * spread
    if len(cuts) > 0:
        array = steps_of(stream_key, extent, cuts, -0.22, 0.18) * array
    return jnp.clip(array, min=-limit, max=limit).astype(kind)


def setup_inputs(seed: int = 0) -> dict:
    streams_of = jax.random.split(jax.random.key(seed), 13)
    return {
        "tokens": normal_values(streams_of[0], (TOKENS, D), 1.0, 6.0, ((0, 32),)),
        "qkv_weight": normal_values(streams_of[1], (3, D, HEADS * HEAD_DIM), D ** -0.5, 0.21875, ((2, 4),)),
        "out_proj": normal_values(streams_of[2], (HEADS * HEAD_DIM, D), (HEADS * HEAD_DIM // 16) ** -0.5, 0.875, ((0, 4),)),
        "rel_bias": normal_values(streams_of[3], (HEADS, BUCKETS), 1.0, 6.0, ((0, 4),), jnp.float32),
        "gains": jnp.clip(1.0 + 0.1 * jax.random.normal(streams_of[4], (2, D), jnp.float32), 0.5, 1.5),
        "router": normal_values(streams_of[5], (D, EXPERTS), (4 * D) ** -0.5, 0.109375),
        "w_in": normal_values(streams_of[6], (EXPERTS, D, FF), D ** -0.5, 0.21875, ((0, 32), (2, 4))),
        "w_out": normal_values(streams_of[7], (EXPERTS, FF, D), (1.4 * EXPERTS * (FF // 2) ** -0.5), 7.0, ((0, 32), (1, 4))),
        "route": draw_route(jax.random.fold_in(streams_of[12], 71), 0),
        "slot": draw_slot(jax.random.fold_in(streams_of[12], 71), 0),
        "buckets": draw_buckets(jax.random.fold_in(streams_of[12], 71), 0),
        "cotangent": normal_values(streams_of[11], (TOKENS, D), 1.0, 6.0, ((0, 32),)),
    }


EPS = 1e-06

@jax.custom_vjp
def low(v):
    return lax.optimization_barrier(v.astype(jnp.bfloat16)).astype(jnp.float32)

@jax.custom_vjp
def low_back(v):
    return v

def low_keep(v):
    return (low(v), None)

def low_pass(kept, grad):
    return (grad,)

def back_keep(v):
    return (v, None)

def back_low(kept, grad):
    return (low(grad),)
low.defvjp(low_keep, low_pass)
low_back.defvjp(back_keep, back_low)

def normalize(values, gain_vec):
    return values * lax.rsqrt(lax.optimization_barrier(jnp.mean(values * values, axis=-1, keepdims=True)) + EPS) * gain_vec

def forward(inputs, qkv_weight, out_proj, rel_bias, gains, router, w_in, w_out, route, slot, buckets):
    highest = lax.Precision.HIGHEST
    normed = low(normalize(inputs, gains[0]))
    positions = jnp.arange(LEN, dtype=jnp.int32)
    offsets = positions[None, :] - positions[:, None] + (LEN - 1)
    full_bias = rel_bias[:, buckets][:, offsets]

    def attend(sequence):
        projected = low_back(low(jnp.einsum('td,cde->cte', sequence, qkv_weight, precision=highest)))
        queries = projected[0].reshape(LEN, HEADS, HEAD_DIM)
        key_rows = projected[1].reshape(LEN, HEADS, HEAD_DIM)
        val_rows = projected[2].reshape(LEN, HEADS, HEAD_DIM)
        scores = jnp.einsum('qhd,khd->hqk', queries, key_rows, precision=highest) * HEAD_DIM ** (-0.5)
        scores = low_back(scores + full_bias)
        weights = low(jax.nn.softmax(scores, axis=-1))
        head_mix = jnp.einsum('hqk,khd->qhd', weights, val_rows, precision=highest).reshape(LEN, HEADS * HEAD_DIM)
        return jnp.dot(low_back(low(head_mix)), out_proj, precision=highest)
    attention = lax.map(jax.checkpoint(attend), normed.reshape(-1, LEN, D)).reshape(-1, D)
    hidden = inputs + low_back(attention)
    mixed = low(normalize(hidden, gains[1]))
    logits = jnp.dot(mixed, router, precision=highest)
    router_probs = jax.nn.softmax(logits, axis=-1)
    gate_prob = jnp.take_along_axis(router_probs, route[:, None], axis=1)
    dispatched = low_back(mixed)
    groups = jnp.arange(route.shape[0], dtype=jnp.int32) // LEN
    row_pos = (groups * CAP + slot).astype(jnp.int32)
    buffer = jnp.zeros((EXPERTS, N_EXPERT * CAP, D), jnp.float32).at[route, row_pos].set(dispatched)

    def expert_apply(operands):
        rows, first, second = operands
        pre_act = low_back(jnp.dot(rows, first, precision=highest))
        activated = low(jax.nn.gelu(pre_act))
        return jnp.dot(activated, second, precision=highest)
    outputs = lax.map(jax.checkpoint(expert_apply), (buffer, w_in, w_out))
    returned = low_back(low(outputs))[route, row_pos]
    return hidden + gate_prob * returned

def reference(tokens, qkv_weight, out_proj, rel_bias, gains, router, w_in, w_out, route, slot, buckets, cotangent):

    def wrapped(inputs, qkv_f, out_f, bias_f, gains_f, router_f, w_in_f, w_out_f):
        return forward(inputs, qkv_f, out_f, bias_f, gains_f, router_f, w_in_f, w_out_f, route, slot, buckets)
    result, pullback = jax.vjp(wrapped, tokens.astype(jnp.float32), qkv_weight.astype(jnp.float32), out_proj.astype(jnp.float32), rel_bias.astype(jnp.float32), gains.astype(jnp.float32), router.astype(jnp.float32), w_in.astype(jnp.float32), w_out.astype(jnp.float32))
    grads = pullback(cotangent.astype(jnp.float32))
    return (result.astype(jnp.bfloat16), grads[0].astype(jnp.bfloat16), grads[1], grads[2], grads[3], grads[4], grads[5], grads[6], grads[7])
```

```python
import jax
import jax.numpy as jnp
from jax import lax
from jax.experimental import pallas as pl
from jax.experimental.pallas import tpu as pltpu
from jax.sharding import PartitionSpec as P

EPS = 1e-06
T = 512
D = 768
NH = 3
HD = 64
W = NH * HD
NE = 32
CAP = 24
SLOTS = NE * CAP
NS = 4
SCALE = HD ** (-0.5)
f32 = jnp.float32
b16 = jnp.bfloat16

NN = (((1,), (0,)), ((), ()))
NT = (((1,), (1,)), ((), ()))
TN = (((0,), (0,)), ((), ()))


def dot(a, b, dims=NN):
    return lax.dot_general(a, b, dims, preferred_element_type=f32)


def call(body, outs, *args, name, flops=0, smem=(), scratch=(), grid=None, in_specs=None, out_specs=None):
    outs = [jax.ShapeDtypeStruct(s, t) for s, t in outs]
    if in_specs is None:
        in_specs = [
            pl.BlockSpec(memory_space=pltpu.SMEM if i in smem else pltpu.VMEM) for i in range(len(args))
        ]
        out_specs = [pl.BlockSpec(memory_space=pltpu.VMEM) for _ in outs]
    size = sum(a.size * a.dtype.itemsize for a in args) + sum(o.size * o.dtype.itemsize for o in outs)
    return pl.pallas_call(
        body,
        out_shape=outs,
        grid=grid or (),
        in_specs=in_specs,
        out_specs=out_specs,
        scratch_shapes=list(scratch),
        compiler_params=pltpu.CompilerParams(vmem_limit_bytes=48 * 1024 * 1024),
        cost_estimate=pl.CostEstimate(flops=flops, bytes_accessed=size, transcendentals=0),
        name=name,
    )(*args)


def lanes(shape):
    return lax.broadcasted_iota(jnp.int32, shape, len(shape) - 1)


def rows_of(shape):
    return lax.broadcasted_iota(jnp.int32, shape, len(shape) - 2)


def roll_half(v):
    return pltpu.roll(v, 64, v.ndim - 1)


def inv_rms(v):
    return lax.rsqrt(jnp.mean(v * v, axis=-1, keepdims=True) + EPS)


def toeplitz_rows(offsets_row, rows, shift):
    wide = jnp.broadcast_to(offsets_row, (rows, offsets_row.shape[1]))
    return pltpu.roll(wide, shift, 1, stride=1, stride_axis=0)


def bucket_hot(bk):
    return (bk == rows_of((NE, 1024))).astype(f32)


def pack_rows(block, half):
    low = lanes((T // 2, 128)) < 64
    tail = jnp.where(low, half[: T // 2], roll_half(half[T // 2 :]))
    return jnp.concatenate([block, tail], axis=0).astype(b16)


def unpack_rows(pieces):
    low = lanes((T // 2, 128)) < 64
    blocks = [p[:T] for p in pieces]
    for left, right in ((0, 1), (2, 3)):
        l_half = pieces[left][T:].astype(f32)
        r_half = pieces[right][T:].astype(f32)
        top = jnp.where(low, l_half, roll_half(r_half))
        bottom = jnp.where(low, roll_half(l_half), r_half)
        blocks.append(jnp.concatenate([top, bottom], axis=0).astype(b16))
    return jnp.concatenate(blocks, axis=1)


def order_pieces(me, refs, held):
    for d, ref in enumerate(refs):
        held[pl.ds(lax.rem(me + (NS - d), NS), 1)] = ref[...][None]


def dispatch_body(idx, val, out):
    hot = (idx[...] == rows_of((SLOTS, T))).astype(b16)
    out[...] = dot(hot, val[...]).reshape(NE, CAP, D).astype(b16)


def attend_body(tok, gains, w, rb, bk, heads, heads_t, a_out, qk_t, v_out, p_out):
    x = tok[...].astype(f32)
    a = (x * inv_rms(x) * gains[0:1, :]).astype(b16)
    a_out[...] = a
    q = dot(a, w[0])
    k = dot(a, w[1])
    v = dot(a, w[2])
    q_t = q.T.astype(b16)
    k_t = k.T.astype(b16)
    v_t = v.T.astype(b16)
    k = k.astype(b16)
    qk_t[0] = q_t
    qk_t[1] = k_t
    v_out[...] = v.astype(b16)
    off = lax.dot_general(rb[...], bucket_hot(bk[...]), NN, precision=lax.Precision.HIGHEST, preferred_element_type=f32)
    outs = []
    for h in range(NH):
        part = slice(HD * h, HD * h + HD)
        s = dot(k[:, part], q_t[part]) * SCALE
        wide = toeplitz_rows(off[h : h + 1], 128, 897)
        bias = jnp.concatenate([wide[:, 384 - 128 * b : 896 - 128 * b] for b in range(4)], axis=0)
        s = s + bias
        e = jnp.exp(s - jnp.max(s, axis=0, keepdims=True))
        p = e / jnp.sum(e, axis=0, keepdims=True)
        p_out[h] = p
        outs.append(dot(v_t[part], p.astype(b16)))
    heads_t[...] = jnp.concatenate(outs, axis=0).astype(b16)
    block = jnp.concatenate(outs[:2], axis=0).T
    tail = jnp.concatenate([outs[2][:, : T // 2], outs[2][:, T // 2 :]], axis=0).T
    heads[...] = jnp.concatenate([block, tail], axis=0).astype(b16)


def order_weights_body(me, w0, w1, w2, w3, out, held):
    order_pieces(me[0], (w0, w1, w2, w3), held)
    parts = [held[j, :128] for j in range(NS)] + [held[j, 128:] for j in range(NS)]
    out[...] = jnp.concatenate(parts, axis=0)


def mix_body(me, idx, tok, gains, h0, h1, h2, h3, w, rows, u_out, hidden_out, held):
    order_pieces(me[0], (h0, h1, h2, h3), held)
    full = unpack_rows([held[j] for j in range(NS)])
    hidden = tok[...].astype(f32) + dot(full, w[...])
    u = (hidden * inv_rms(hidden) * gains[1:2, :]).astype(b16)
    hot = (idx[...] == rows_of((SLOTS, T))).astype(b16)
    rows[...] = dot(hot, u).reshape(NE, CAP, D).astype(b16)
    u_out[...] = u
    hidden_out[...] = hidden


def gate_body(u, router, route, gate_out, coef_out, coef_router_out):
    logits = dot(u[...], router[...])
    e = jnp.exp(logits - jnp.max(logits, axis=1, keepdims=True))
    probs = e / jnp.sum(e, axis=1, keepdims=True)
    chosen = (route[...] == lanes((T, NE))).astype(f32)
    gate = jnp.sum(probs * chosen, axis=1, keepdims=True)
    coef = probs * (chosen - gate)
    high = coef.astype(b16)
    low = (coef - high.astype(f32)).astype(b16)
    gate_out[...] = gate
    coef_out[...] = coef
    coef_router_out[...] = dot(high, router[...], NT) + dot(low, router[...], NT)


def ungated_body(g, w_out, h):
    h[...] = dot(g[...], w_out[...], NT)


def pack_return(val, extra, out):
    n = val.shape[0] // CAP
    low = lanes((n, 8, 128)) < 64
    if extra is not None:
        ext = extra.reshape(n, CAP, 1)
        hi = ext.astype(b16).astype(f32)
        lo = ext - hi
        lane = lanes((n, 8, 128))
        tail = jnp.zeros((n, 8, 128), f32)
        for t in range(3):
            tail = jnp.where(lane == 64 + t, hi[:, 8 * t : 8 * t + 8], tail)
            tail = jnp.where(lane == 67 + t, lo[:, 8 * t : 8 * t + 8], tail)
    else:
        tail = jnp.zeros((n, 8, 128), f32)
    res = []
    for s in range(NS):
        block = val[:, 128 * s : 128 * s + 128].reshape(n, CAP, 128)
        c = 512 + 128 * (s // 2)
        half = val[:, c : c + 128].reshape(n, CAP, 128)
        moved = roll_half(half)
        x0, x1, x2 = (half[:, 8 * t : 8 * t + 8] for t in range(3))
        r0, r1, r2 = (moved[:, 8 * t : 8 * t + 8] for t in range(3))
        if s % 2 == 0:
            t3, t4 = jnp.where(low, x0, r1), jnp.where(low, x2, tail)
        else:
            t3, t4 = jnp.where(low, r0, x1), jnp.where(low, r2, tail)
        res.append(jnp.concatenate([block, t3, t4], axis=1))
    out[...] = jnp.stack(res, axis=1).astype(b16)


GELU_C = 0.7978845608028654


def expert_body(me, rows, h, w_in, router, ret, act_out, dpre_out, gate_out):
    u = rows[...]
    logits = dot(u, router[...])
    e = jnp.exp(logits - jnp.max(logits, axis=1, keepdims=True))
    mine = (lanes(logits.shape) == me[0]).astype(f32)
    gate = jnp.sum(e * mine, axis=1, keepdims=True) / jnp.sum(e, axis=1, keepdims=True)
    pre = dot(u, w_in[...])
    sq = pre * pre
    th = jnp.tanh(GELU_C * pre * (1.0 + 0.044715 * sq))
    act = (0.5 * pre * (1.0 + th)).astype(b16)
    slope = 0.5 * (1.0 + th) + 0.5 * pre * (1.0 - th * th) * (GELU_C * (1.0 + 3 * 0.044715 * sq))
    hv = h[...]
    d_gate = jnp.sum(act.astype(f32) * hv, axis=1, keepdims=True)
    d_pre = (gate * hv * slope).astype(b16)
    act_out[...] = act
    dpre_out[...] = d_pre
    gate_out[...] = gate
    pack_return(dot(d_pre, w_in[...], NT), d_gate, ret)


def value_body(act, w_out, ret):
    pack_return(dot(act[...], w_out[...]), None, ret)


def collect_body(idx, got, piece, *d_gate):
    total = jnp.sum(got[...].astype(f32), axis=1)
    block = total[:, :CAP].reshape(SLOTS, 128).astype(b16)
    t3 = total[:, 24:32]
    t4 = total[:, 32:40]
    half = jnp.concatenate([t3, roll_half(t3), t4], axis=1).reshape(SLOTS, 128)
    lane = lanes((SLOTS, 128))
    if d_gate:
        tl = lanes(t4.shape)
        cols = []
        for t in range(3):
            cols.append(jnp.sum(jnp.where((tl == 64 + t) | (tl == 67 + t), t4, 0.0), axis=2, keepdims=True))
        col = jnp.concatenate(cols, axis=1).reshape(SLOTS, 1)
        hi = col.astype(b16).astype(f32)
        half = jnp.where(lane < 64, half, jnp.where(lane == 64, hi, jnp.where(lane == 65, col - hi, 0.0)))
    else:
        half = jnp.where(lane < 64, half, 0.0)
    hot = (idx[...] == lanes((T, SLOTS))).astype(b16)
    mine = dot(hot, jnp.concatenate([block, half.astype(b16)], axis=1))
    piece[...] = pack_rows(mine[:, :128], mine[:, 128:])
    if d_gate:
        lt = lanes((T, 128))
        d_gate[0][...] = jnp.sum(
            jnp.where((lt == 64) | (lt == 65), mine[:, 128:], 0.0), axis=1, keepdims=True
        )


def backward_body(
    me, p0, p1, p2, p3, d_gate, coef, coef_router, u, cot, hidden_in, gains, out_proj, heads_t, a, qk_t, v, p, w, bk,
    pay, da_out, dhid_out, held, scr,
):
    order_pieces(me[0], (p0, p1, p2, p3), held)
    d_expert = unpack_rows([held[j] for j in range(NS)]).astype(f32)
    dg = d_gate[...]
    d_u = dg * coef_router[...] + d_expert
    hidden = hidden_in[...]
    r2 = inv_rms(hidden)
    n2 = hidden * r2
    gain_two = jnp.sum(d_u * n2, axis=0, keepdims=True)
    v2 = d_u * gains[1:2, :]
    d_hidden = cot[...].astype(f32) + r2 * (v2 - n2 * jnp.mean(v2 * n2, axis=-1, keepdims=True))
    dhid_out[...] = d_hidden
    d_att = d_hidden.astype(b16)
    d_logits = coef[...] * dg
    high = d_logits.astype(b16)
    low = (d_logits - high.astype(f32)).astype(b16)
    router_t = dot(high, u[...], TN) + dot(low, u[...], TN)
    g_out = dot(heads_t[...], d_att)
    do_t = dot(out_proj[...], d_att, NT).astype(b16)
    hot = bucket_hot(bk[...])
    dqs, dks, dvs, bias = [], [], [], []
    for h in range(NH):
        part = slice(HD * h, HD * h + HD)
        prob = p[h]
        dp = dot(v[:, part], do_t[part])
        delta = jnp.sum(prob * dp, axis=0, keepdims=True)
        ds = (prob * (dp - delta)).astype(b16)
        dvs.append(dot(do_t[part], prob.astype(b16), NT))
        dks.append(dot(qk_t[0, part], ds, NT) * SCALE)
        dqs.append(dot(qk_t[1, part], ds) * SCALE)
        ds_f = ds.astype(f32)
        acc = jnp.zeros((128, 1024), f32)
        for b in range(4):
            left, right = 384 - 128 * b, 128 + 128 * b
            blk = ds_f[128 * b : 128 * b + 128]
            parts = ([jnp.zeros((128, left), f32)] if left else []) + [blk, jnp.zeros((128, right), f32)]
            acc = acc + jnp.concatenate(parts, axis=1)
        acc = pltpu.roll(acc, 127, 1)
        row = rows_of((128, 1024))
        for bit in range(7):
            step = 1 << bit
            acc = jnp.where((row & step) != 0, pltpu.roll(acc, 1024 - step, 1), acc)
        bias.append(jnp.sum(acc, axis=0, keepdims=True))
    bias = lax.dot_general(
        jnp.concatenate(bias + [jnp.zeros((5, 1024), f32)], axis=0), hot, NT,
        precision=lax.Precision.HIGHEST, preferred_element_type=f32,
    )
    dq = jnp.concatenate(dqs, axis=0).astype(b16)
    dk = jnp.concatenate(dks, axis=0).astype(b16)
    dv = jnp.concatenate(dvs, axis=0).astype(b16)
    da = dot(w[0], dq) + dot(w[1], dk) + dot(w[2], dv)
    a_v = a[...]
    grads = [dot(m, a_v) for m in (dq, dk, dv)]
    gain_rows = [
        jnp.sum(w[c].astype(f32).T * grads[c], axis=0, keepdims=True) for c in range(3)
    ]
    gain_one = gain_rows[0] + gain_rows[1] + gain_rows[2]
    full = jnp.concatenate(grads + [g_out], axis=0)
    for l in range(6):
        cut = slice(128 * l, 128 * l + 128)
        scr[:, 24 * l : 24 * l + 24, :] = full[:, cut].reshape(NE, CAP, 128)
        scr[:, 144 + l, :] = router_t[:, cut]
    scr[:, 150:152, :] = jnp.zeros((NE, 2, 128), f32)
    for l in range(6):
        scr[l, 150:151, :] = gain_two[:, 128 * l : 128 * l + 128]
    wide = jnp.concatenate([bias, jnp.zeros((8, 96), f32)], axis=1)
    for h in range(NH):
        scr[6 + h, 150:151, :] = wide[h : h + 1]
    pay[...] = scr[...].astype(b16)
    gl = jnp.concatenate(
        [gain_one[:, 128 * l : 128 * l + 128] for l in range(6)] + [jnp.zeros((2, 128), f32)], axis=0
    )
    hi = gl.astype(b16).astype(f32)
    gl = jnp.concatenate([hi, gl - hi], axis=0)
    for s in range(NS):
        da_out[s] = jnp.concatenate([da[:, 128 * s : 128 * s + 128], gl], axis=0).astype(b16)


def sum_body(pay, da, out):
    total = jnp.sum(pay[...].astype(f32), axis=0)
    gl = jnp.sum(da[:, D:, :].astype(f32), axis=0)
    chunk = jnp.concatenate([total, gl[:8] + gl[8:]], axis=0).astype(b16)
    out[...] = jnp.broadcast_to(chunk[None], (NE, 160, 128))


def token_grad_body(me, da, tok, dhid, gains, out):
    d_a = jnp.sum(da[:, :D, :].astype(f32), axis=0).T
    at = pl.ds(pl.multiple_of(me[0] * 128, 128), 128)
    x = tok[at, :].astype(f32)
    r1 = inv_rms(x)
    n1 = x * r1
    v1 = d_a * gains[0:1, :]
    out[...] = (dhid[at, :] + r1 * (v1 - n1 * jnp.mean(v1 * n1, axis=-1, keepdims=True))).astype(b16)


def join_body(me, t0, t1, t2, t3, out):
    for d, ref in enumerate((t0, t1, t2, t3)):
        src = lax.rem(me[0] + (NS - d), NS)
        out[pl.ds(pl.multiple_of(src * 128, 128), 128), :] = ref[...]


def result_body(me, p0, p1, p2, p3, gate, hidden, out, held):
    order_pieces(me[0], (p0, p1, p2, p3), held)
    value = unpack_rows([held[j] for j in range(NS)]).astype(f32)
    out[...] = (hidden[...] + gate[...] * value).astype(b16)


def finish_body(got, gains, qkv, proj, bias, gains_out, router, scr):
    scr[...] = got[...].astype(f32)
    full = jnp.concatenate([scr[:, 24 * l : 24 * l + 24, :].reshape(D, 128) for l in range(6)], axis=1)
    for c in range(3):
        qkv[c] = full[W * c : W * c + W].T
    proj[...] = full[3 * W :]
    router[...] = jnp.concatenate([scr[:, 144 + l, :] for l in range(6)], axis=1).T
    gl = jnp.sum(scr[:, 152:160, :], axis=0)
    one = jnp.concatenate([gl[l : l + 1] for l in range(6)], axis=1) / gains[0:1, :]
    two = jnp.concatenate([scr[l, 150:151, :] for l in range(6)], axis=1)
    gains_out[...] = jnp.concatenate([one, two], axis=0)
    bias[...] = jnp.concatenate([scr[6 + h, 150:151, :NE] for h in range(NH)], axis=0)


def over_experts(v):
    return lax.all_to_all(v, "expert", split_axis=0, concat_axis=0, tiled=True)


def over_all(v):
    return lax.all_to_all(v, ("expert", "shard"), split_axis=0, concat_axis=0, tiled=True)


def round_shard(v):
    return [v] + [lax.ppermute(v, "shard", [(i, (i + d) % NS) for i in range(NS)]) for d in (1, 2, 3)]


def local(tokens, qkv_weight, out_proj, rel_bias, gains, router, w_in, w_out, route, slot, buckets, cotangent):
    w_in = w_in.reshape(D, -1)
    w_out = w_out.reshape(-1, D)
    ff = w_in.shape[1]
    me = jnp.full((1,), lax.axis_index("shard"), jnp.int32)
    expert = jnp.full((1,), lax.axis_index("expert"), jnp.int32)
    idx = route * CAP + slot
    idx_row = idx[None, :]
    idx_col = idx[:, None]
    bk = jnp.concatenate([jnp.flip(buckets), jnp.full((1,), -1, jnp.int32)])[None, :]

    (g_rows,) = call(dispatch_body, [((NE, CAP, D), b16)], idx_row, cotangent, name="dispatch_cotangent")
    g_rows = over_experts(g_rows).reshape(SLOTS, D)
    w_pieces = round_shard(out_proj)

    heads, heads_t, a, qk_t, v, p = call(
        attend_body,
        [((D, 128), b16), ((W, T), b16), ((T, D), b16), ((2, W, T), b16), ((T, W), b16), ((NH, T, T), f32)],
        tokens, gains, qkv_weight, rel_bias, bk, name="attend",
    )
    h_pieces = round_shard(heads)
    (w_full,) = call(
        order_weights_body, [((D, D), b16)], me, *w_pieces, name="order_weights", smem=(0,),
        scratch=[pltpu.VMEM((NS, W, D), b16)],
    )
    (h,) = call(ungated_body, [((SLOTS, ff), f32)], g_rows, w_out, name="ungated")
    rows, u, hidden = call(
        mix_body,
        [((NE, CAP, D), b16), ((T, D), b16), ((T, D), f32)],
        me, idx_row, tokens, gains, *h_pieces, w_full, name="mix", smem=(0,),
        scratch=[pltpu.VMEM((NS, D, 128), b16)],
    )
    u_rows = over_experts(rows).reshape(SLOTS, D)
    gate, coef, coef_router = call(
        gate_body, [((T, 1), f32), ((T, NE), f32), ((T, D), f32)], u, router, route[:, None], name="gate",
    )
    half = SLOTS // 2
    vm = pltpu.VMEM
    row_spec = lambda n: pl.BlockSpec((half, n), lambda i: (i, 0), memory_space=vm)
    all_spec = lambda s: pl.BlockSpec(s, lambda i: (0,) * len(s), memory_space=vm)
    ret_spec = pl.BlockSpec((NE // 2, NS, 40, 128), lambda i: (i, 0, 0, 0), memory_space=vm)
    ret, act, d_pre, row_gate = call(
        expert_body,
        [((NE, NS, 40, 128), b16), ((SLOTS, ff), b16), ((SLOTS, ff), b16), ((SLOTS, 1), f32)],
        expert, u_rows, h, w_in, router, name="expert", grid=(2,),
        in_specs=[pl.BlockSpec(memory_space=pltpu.SMEM), row_spec(D), row_spec(ff), all_spec((D, ff)), all_spec((D, NE))],
        out_specs=[ret_spec, row_spec(ff), row_spec(ff), row_spec(1)],
    )
    back = over_all(ret.reshape(NE * NS, 40, 128)).reshape(NE, NS, 40, 128)
    (val,) = call(
        value_body, [((NE, NS, 40, 128), b16)], act, w_out, name="value", grid=(2,),
        in_specs=[row_spec(ff), all_spec((ff, D))], out_specs=[ret_spec],
    )
    piece, d_gate = call(
        collect_body, [((D, 128), b16), ((T, 1), f32)], idx_col, back, name="collect_back"
    )
    b_pieces = round_shard(piece)
    value = over_all(val.reshape(NE * NS, 40, 128)).reshape(NE, NS, 40, 128)
    d_rows = (row_gate * g_rows.astype(f32)).astype(b16)
    grad_w_out = dot(act, d_rows, TN)[None]
    grad_w_in = dot(u_rows, d_pre, TN)[None]

    pay, da, d_hidden = call(
        backward_body,
        [((NE, 152, 128), b16), ((NS, D + 16, 128), b16), ((T, D), f32)],
        me, *b_pieces, d_gate, coef, coef_router, u, cotangent, hidden, gains, out_proj, heads_t, a, qk_t, v, p,
        qkv_weight, bk, name="backward", smem=(0,),
        scratch=[pltpu.VMEM((NS, D, 128), b16), pltpu.VMEM((NE, 152, 128), f32)],
    )
    pay = over_experts(pay)
    da = lax.all_to_all(da, "shard", split_axis=0, concat_axis=0, tiled=True)
    (chunk,) = call(sum_body, [((NE, 160, 128), b16)], pay, da, name="sum_gradients")
    chunk = over_experts(chunk)
    (t_piece,) = call(token_grad_body, [((128, D), b16)], me, da, tokens, d_hidden, gains, name="token_grad", smem=(0,))
    (grad_tokens,) = call(join_body, [((T, D), b16)], me, *round_shard(t_piece), name="join_tokens", smem=(0,))
    (v_piece,) = call(collect_body, [((D, 128), b16)], idx_col, value, name="collect_value")
    (result,) = call(
        result_body, [((T, D), b16)], me, *round_shard(v_piece), gate, hidden, name="result", smem=(0,),
        scratch=[pltpu.VMEM((NS, D, 128), b16)],
    )
    grad_qkv, grad_proj, grad_bias, grad_gains, grad_router = call(
        finish_body,
        [((3, D, W), f32), ((W, D), f32), ((NH, NE), f32), ((2, D), f32), ((D, NE), f32)],
        chunk, gains, name="finish", scratch=[pltpu.VMEM((NE, 160, 128), f32)],
    )
    return result, grad_tokens, grad_qkv, grad_proj, grad_bias, grad_gains, grad_router, grad_w_in, grad_w_out


def solution(mesh):
    in_specs = (
        P("expert", None),
        P(None, None, "shard"),
        P("shard", None),
        P("shard", None),
        P(),
        P(),
        P("expert", None, "shard"),
        P("expert", "shard", None),
        P("expert"),
        P("expert"),
        P(),
        P("expert", None),
    )
    out_specs = (
        P("expert", None),
        P("expert", None),
        P(None, None, "shard"),
        P("shard", None),
        P("shard", None),
        P(),
        P(),
        P("expert", None, "shard"),
        P("expert", "shard", None),
    )
    return jax.shard_map(local, mesh=mesh, in_specs=in_specs, out_specs=out_specs, check_vma=False)
```

```python
import jax
import jax.numpy as jnp
from jax import lax
from jax.experimental import pallas as pl
from jax.experimental.pallas import tpu as pltpu
from jax.sharding import PartitionSpec as P

EPS = 1e-06
T = 512
D = 768
NH = 3
HD = 64
W = NH * HD
NE = 32
CAP = 24
SLOTS = NE * CAP
NS = 4
SCALE = HD ** (-0.5)
f32 = jnp.float32
b16 = jnp.bfloat16

NN = (((1,), (0,)), ((), ()))
NT = (((1,), (1,)), ((), ()))
TN = (((0,), (0,)), ((), ()))


def dot(a, b, dims=NN):
    return lax.dot_general(a, b, dims, preferred_element_type=f32)


class Place:
    def __init__(self, axis):
        self.axis = axis


class Parts:
    def __init__(self, array):
        self.array = array


class Quarter:
    def __init__(self, array):
        self.array = array


class Pieces:
    def __init__(self, arrays):
        self.arrays = arrays


class Load:
    def __init__(self, held, copies):
        self.held, self.copies = held, copies

    def start(self):
        for c in self.copies:
            c.start()

    def ready(self, at=None):
        for k, c in enumerate(self.copies):
            if c is not None and (at is None or at == k):
                c.wait()
                self.copies[k] = None

    def __getitem__(self, at):
        self.ready()
        return self.held[at]


class LoadParts(Load):
    def __getitem__(self, at):
        self.ready(at if isinstance(at, int) else at[0])
        return self.held[at]


class Store:
    def __init__(self, out, held, sems):
        self.out, self.held, self.sems, self.copies = out, held, sems, []

    def __setitem__(self, at, value):
        self.held[at] = value

    def flush(self, at=None, src=None):
        sem = self.sems.at[len(self.copies)]
        src = self.held if src is None else src
        if at is None:
            copy = pltpu.make_async_copy(src, self.out, sem)
        else:
            copy = pltpu.make_async_copy(src.at[at], self.out.at[at], sem)
        copy.start()
        self.copies.append(copy)

    def finish(self):
        for c in self.copies:
            c.wait()


def call(body, outs, *args, name, scratch=(), unheld=(), room=0):
    outs = [jax.ShapeDtypeStruct(s, t) for s, t in outs]
    hbm = pl.BlockSpec(memory_space=pltpu.HBM)
    flat, in_specs, buffers = [], [], []
    for a in args:
        if isinstance(a, Place):
            continue
        if isinstance(a, Pieces):
            flat += a.arrays
            in_specs += [hbm] * NS
            buffers += [pltpu.VMEM((NS,) + a.arrays[0].shape, a.arrays[0].dtype), pltpu.SemaphoreType.DMA((NS,))]
        elif isinstance(a, Parts):
            flat.append(a.array)
            in_specs.append(hbm)
            buffers += [pltpu.VMEM(a.array.shape, a.array.dtype), pltpu.SemaphoreType.DMA((a.array.shape[0],))]
        elif isinstance(a, Quarter):
            flat.append(a.array)
            in_specs.append(hbm)
            shape = (a.array.shape[0] // NS,) + a.array.shape[1:]
            buffers += [pltpu.VMEM(shape, a.array.dtype), pltpu.SemaphoreType.DMA((1,))]
        else:
            flat.append(a)
            in_specs.append(hbm)
            buffers += [pltpu.VMEM(a.shape, a.dtype), pltpu.SemaphoreType.DMA((1,))]
    for k, o in enumerate(outs):
        if k not in unheld:
            buffers.append(pltpu.VMEM(o.shape, o.dtype))
        buffers.append(pltpu.SemaphoreType.DMA((4,)))

    def kernel(*refs):
        ins = iter(refs[: len(flat)])
        results = refs[len(flat) : len(flat) + len(outs)]
        rest = refs[len(flat) + len(outs) :]
        bufs, user = iter(rest[: len(buffers)]), rest[len(buffers) :]
        given, me = [], None
        for a in args:
            if isinstance(a, Place):
                me = [lax.axis_index(a.axis)]
                given.append(me)
                continue
            if isinstance(a, Pieces):
                held, sems = next(bufs), next(bufs)
                item = Load(held, [
                    pltpu.make_async_copy(next(ins), held.at[lax.rem(me[0] + (NS - d), NS)], sems.at[d])
                    for d in range(NS)
                ])
            elif isinstance(a, Parts):
                ref, held, sems = next(ins), next(bufs), next(bufs)
                item = LoadParts(held, [
                    pltpu.make_async_copy(ref.at[k], held.at[k], sems.at[k]) for k in range(a.array.shape[0])
                ])
            elif isinstance(a, Quarter):
                ref, held, sems = next(ins), next(bufs), next(bufs)
                n = held.shape[0]
                at = pl.ds(pl.multiple_of(me[0] * n, n), n)
                item = Load(held, [pltpu.make_async_copy(ref.at[at], held, sems.at[0])])
            else:
                ref, held, sems = next(ins), next(bufs), next(bufs)
                item = Load(held, [pltpu.make_async_copy(ref, held, sems.at[0])])
            item.start()
            given.append(item)
        stores = []
        for k, out in enumerate(results):
            held = None if k in unheld else next(bufs)
            stores.append(Store(out, held, next(bufs)))
        body(*given, *stores, *user)
        for item in given:
            if isinstance(item, Load):
                item.ready()
        for item in stores:
            if not item.copies:
                item.flush()
        for item in stores:
            item.finish()

    return pl.pallas_call(
        kernel,
        out_shape=outs,
        in_specs=in_specs,
        out_specs=[hbm] * len(outs),
        scratch_shapes=buffers + list(scratch),
        compiler_params=pltpu.CompilerParams(vmem_limit_bytes=(60 - room) * 1024 * 1024),
        cost_estimate=pl.CostEstimate(flops=0, bytes_accessed=300000, transcendentals=0),
        name=name,
    )(*flat)


def lanes(shape):
    return lax.broadcasted_iota(jnp.int32, shape, len(shape) - 1)


def rows_of(shape):
    return lax.broadcasted_iota(jnp.int32, shape, len(shape) - 2)


def roll_half(v):
    return pltpu.roll(v, 64, v.ndim - 1)


def inv_rms(v):
    return lax.rsqrt(jnp.mean(v * v, axis=-1, keepdims=True) + EPS)


def toeplitz_rows(offsets_row, rows, shift):
    wide = jnp.broadcast_to(offsets_row, (rows, offsets_row.shape[1]))
    return pltpu.roll(wide, shift, 1, stride=1, stride_axis=0)


def bucket_hot(bk):
    return (bk == rows_of((NE, 1024))).astype(f32)


def pack_rows(block, half):
    low = lanes((T // 2, 128)) < 64
    tail = jnp.where(low, half[: T // 2], roll_half(half[T // 2 :]))
    return jnp.concatenate([block, tail], axis=0).astype(b16)


def unpack_rows(pieces):
    low = lanes((T // 2, 128)) < 64
    blocks = [p[:T] for p in pieces]
    for left, right in ((0, 1), (2, 3)):
        l_half = pieces[left][T:].astype(f32)
        r_half = pieces[right][T:].astype(f32)
        top = jnp.where(low, l_half, roll_half(r_half))
        bottom = jnp.where(low, roll_half(l_half), r_half)
        blocks.append(jnp.concatenate([top, bottom], axis=0).astype(b16))
    return jnp.concatenate(blocks, axis=1)


def dispatch_body(route, slot, val, out):
    hot = (route[...] * CAP + slot[...] == rows_of((SLOTS, T))).astype(b16)
    out[...] = dot(hot, val[...]).reshape(NE, CAP, D).astype(b16)


def attend_body(tok, gains, w, rb, bk, heads, heads_t, a_out, qk_t, v_out, p_out):
    x = tok[...].astype(f32)
    a = (x * inv_rms(x) * gains[0:1, :]).astype(b16)
    a_out[...] = a
    a_out.flush()
    q_t = dot(w[0], a, NT).astype(b16)
    v_t = dot(w[2], a, NT).astype(b16)
    k = dot(a, w[1], NT).astype(b16)
    qk_t[0] = q_t
    qk_t[1] = dot(w[1], a, NT).astype(b16)
    qk_t.flush()
    v_out[...] = dot(a, w[2], NT).astype(b16)
    v_out.flush()
    off = lax.dot_general(rb[...], bucket_hot(bk[...]), NN, precision=lax.Precision.HIGHEST, preferred_element_type=f32)
    outs = []
    for h in range(NH):
        part = slice(HD * h, HD * h + HD)
        s = dot(k[:, part], q_t[part]) * SCALE
        wide = toeplitz_rows(off[h : h + 1], 128, 897)
        bias = jnp.concatenate([wide[:, 384 - 128 * b : 896 - 128 * b] for b in range(4)], axis=0)
        s = s + bias
        e = jnp.exp(s - jnp.max(s, axis=0, keepdims=True))
        p = e / jnp.sum(e, axis=0, keepdims=True)
        p_out[h] = p
        p_out.flush(h)
        outs.append(dot(v_t[part], p.astype(b16)))
    heads_t[...] = jnp.concatenate(outs, axis=0).astype(b16)
    block = jnp.concatenate(outs[:2], axis=0).T
    tail = jnp.concatenate([outs[2][:, : T // 2], outs[2][:, T // 2 :]], axis=0).T
    heads[...] = jnp.concatenate([block, tail], axis=0).astype(b16)


def order_weights_body(me, held, out):
    parts = [held[j, :128] for j in range(NS)] + [held[j, 128:] for j in range(NS)]
    out[...] = jnp.concatenate(parts, axis=0)


def mix_body(me, route, slot, gains, held, w, tok, rows, u_out, hidden_out):
    full = unpack_rows([held[j] for j in range(NS)])
    hidden = tok[...].astype(f32) + dot(full, w[...])
    u = (hidden * inv_rms(hidden) * gains[1:2, :]).astype(b16)
    hidden_out[...] = hidden
    hidden_out.flush()
    u_out[...] = u
    u_out.flush()
    hot = (route[...] * CAP + slot[...] == rows_of((SLOTS, T))).astype(b16)
    rows[...] = dot(hot, u).reshape(NE, CAP, D).astype(b16)


def gate_body(u, router, route, gate_out, coef_out):
    logits = dot(u[...], router[...], NT)
    e = jnp.exp(logits - jnp.max(logits, axis=1, keepdims=True))
    probs = e / jnp.sum(e, axis=1, keepdims=True)
    chosen = (route[...] == lanes((T, NE))).astype(f32)
    gate = jnp.sum(probs * chosen, axis=1, keepdims=True)
    coef = probs * (chosen - gate)
    gate_out[...] = gate
    coef_out[...] = coef


def ungated_body(g, w_out, h):
    h[...] = dot(g[...], w_out[...], NT)


def pack_return(val, extra=None):
    n = val.shape[0] // CAP
    low = lanes((n, 8, 128)) < 64
    if extra is not None:
        ext = extra.reshape(n, CAP, 1)
        hi = ext.astype(b16).astype(f32)
        lo = ext - hi
        lane = lanes((n, 8, 128))
        tail = jnp.zeros((n, 8, 128), f32)
        for t in range(3):
            tail = jnp.where(lane == 64 + t, hi[:, 8 * t : 8 * t + 8], tail)
            tail = jnp.where(lane == 67 + t, lo[:, 8 * t : 8 * t + 8], tail)
    else:
        tail = jnp.zeros((n, 8, 128), f32)
    res = []
    for s in range(NS):
        block = val[:, 128 * s : 128 * s + 128].reshape(n, CAP, 128)
        c = 512 + 128 * (s // 2)
        half = val[:, c : c + 128].reshape(n, CAP, 128)
        moved = roll_half(half)
        x0, x1, x2 = (half[:, 8 * t : 8 * t + 8] for t in range(3))
        r0, r1, r2 = (moved[:, 8 * t : 8 * t + 8] for t in range(3))
        if s % 2 == 0:
            t3, t4 = jnp.where(low, x0, r1), jnp.where(low, x2, tail)
        else:
            t3, t4 = jnp.where(low, r0, x1), jnp.where(low, r2, tail)
        res.append(jnp.concatenate([block, t3, t4], axis=1))
    return [r.astype(b16) for r in res]


PAY = 152

GELU_C = 0.7978845608028654


def expert_body(me, router, rows, w_in, h, ret, act_out, dpre_out, gate_out):
    half = SLOTS // 2
    for i in range(2):
        cut = slice(half * i, half * i + half)
        seqs = slice(NE // 2 * i, NE // 2 * (i + 1))
        u = rows[cut, :]
        logits = dot(u, router[...], NT)
        e = jnp.exp(logits - jnp.max(logits, axis=1, keepdims=True))
        mine = (lanes(logits.shape) == me[0]).astype(f32)
        gate = jnp.sum(e * mine, axis=1, keepdims=True) / jnp.sum(e, axis=1, keepdims=True)
        pre = dot(u, w_in[...])
        sq = pre * pre
        th = jnp.tanh(GELU_C * pre * (1.0 + 0.044715 * sq))
        act = (0.5 * pre * (1.0 + th)).astype(b16)
        slope = 0.5 * (1.0 + th) + 0.5 * pre * (1.0 - th * th) * (GELU_C * (1.0 + 3 * 0.044715 * sq))
        hv = h[cut, :]
        d_gate = jnp.sum(act.astype(f32) * hv, axis=1, keepdims=True)
        d_pre = (gate * hv * slope).astype(b16)
        grads = pack_return(dot(d_pre, w_in[...], NT), d_gate)
        for s in range(NS):
            ret[seqs, s] = grads[s]
        ret.flush(seqs)
        act_out[cut, :] = act
        dpre_out[cut, :] = d_pre
        gate_out[cut, :] = gate


def value_body(act, w_out, ret):
    half = SLOTS // 2
    for i in range(2):
        values = pack_return(dot(act[half * i : half * i + half, :], w_out[...]))
        seqs = slice(NE // 2 * i, NE // 2 * (i + 1))
        for s in range(NS):
            ret[seqs, s] = values[s]
        ret.flush(seqs)


def unpack_return(total):
    block = total[:, :CAP].reshape(SLOTS, 128).astype(b16)
    t3 = total[:, 24:32]
    t4 = total[:, 32:40]
    return block, jnp.concatenate([t3, roll_half(t3), t4], axis=1).reshape(SLOTS, 128), t4


def collect_body(route, slot, got, piece, d_gate):
    block, half, t4 = unpack_return(jnp.sum(got[...].astype(f32), axis=1))
    lane = lanes((SLOTS, 128))
    tl = lanes(t4.shape)
    cols = []
    for t in range(3):
        cols.append(jnp.sum(jnp.where((tl == 64 + t) | (tl == 67 + t), t4, 0.0), axis=2, keepdims=True))
    col = jnp.concatenate(cols, axis=1).reshape(SLOTS, 1)
    hi = col.astype(b16).astype(f32)
    half = jnp.where(lane < 64, half, jnp.where(lane == 64, hi, jnp.where(lane == 65, col - hi, 0.0)))
    hot = (route[...] * CAP + slot[...] == lanes((T, SLOTS))).astype(b16)
    mine = dot(hot, jnp.concatenate([block, half.astype(b16)], axis=1))
    piece[...] = pack_rows(mine[:, :128], mine[:, 128:])
    piece.flush()
    lt = lanes((T, 128))
    d_gate[...] = jnp.sum(jnp.where((lt == 64) | (lt == 65), mine[:, 128:], 0.0), axis=1, keepdims=True)


def collect_value_body(route, slot, got, value):
    block, half, _ = unpack_return(jnp.sum(got[...].astype(f32), axis=1))
    half = jnp.where(lanes(half.shape) < 64, half, 0.0)
    hot = (route[...] * CAP + slot[...] == lanes((T, SLOTS))).astype(b16)
    mine = dot(hot, jnp.concatenate([block, half.astype(b16)], axis=1))
    value[...] = pack_rows(mine[:, :128], mine[:, 128:])


def backward_body(
    me, gains, d_gate, coef, router, held, hidden_in, cot, out_proj, v, p, qk_t, heads_t, u, a, bk, w,
    pay, d_proj, gain_out, dhid_out, scr, dhid,
):
    d_expert = unpack_rows([held[j] for j in range(NS)]).astype(f32)
    dg = d_gate[...]
    d_logits = coef[...] * dg
    high = d_logits.astype(b16)
    low = (d_logits - high.astype(f32)).astype(b16)
    d_u = dot(high, router[...]) + dot(low, router[...]) + d_expert
    hidden = hidden_in[...]
    r2 = inv_rms(hidden)
    n2 = hidden * r2
    gain_two = jnp.sum(d_u * n2, axis=0, keepdims=True)
    v2 = d_u * gains[1:2, :]
    d_hidden = cot[...].astype(f32) + r2 * (v2 - n2 * jnp.mean(v2 * n2, axis=-1, keepdims=True))
    dhid[...] = d_hidden
    dhid_out.flush(src=dhid.at[pl.ds(pl.multiple_of(me[0] * 128, 128), 128)])
    d_att = d_hidden.astype(b16)
    router_t = dot(high, u[...], TN) + dot(low, u[...], TN)
    g_out = dot(heads_t[...], d_att)
    do_t = dot(out_proj[...], d_att, NT).astype(b16)
    hot = bucket_hot(bk[...])
    dqs, dks, dvs, bias = [], [], [], []
    for h in range(NH):
        part = slice(HD * h, HD * h + HD)
        prob = p[h]
        dp = dot(v[:, part], do_t[part])
        delta = jnp.sum(prob * dp, axis=0, keepdims=True)
        ds = (prob * (dp - delta)).astype(b16)
        dvs.append(dot(do_t[part], prob.astype(b16), NT))
        dks.append(dot(qk_t[0, part], ds, NT) * SCALE)
        dqs.append(dot(qk_t[1, part], ds) * SCALE)
        ds_f = ds.astype(f32)
        acc = jnp.zeros((128, 1024), f32)
        for b in range(4):
            left, right = 384 - 128 * b, 128 + 128 * b
            blk = ds_f[128 * b : 128 * b + 128]
            parts = ([jnp.zeros((128, left), f32)] if left else []) + [blk, jnp.zeros((128, right), f32)]
            acc = acc + jnp.concatenate(parts, axis=1)
        acc = pltpu.roll(acc, 127, 1)
        row = rows_of((128, 1024))
        for bit in range(7):
            step = 1 << bit
            acc = jnp.where((row & step) != 0, pltpu.roll(acc, 1024 - step, 1), acc)
        bias.append(jnp.sum(acc, axis=0, keepdims=True))
    bias = lax.dot_general(
        jnp.concatenate(bias + [jnp.zeros((5, 1024), f32)], axis=0), hot, NT,
        precision=lax.Precision.HIGHEST, preferred_element_type=f32,
    )
    dq = jnp.concatenate(dqs, axis=0).astype(b16)
    dk = jnp.concatenate(dks, axis=0).astype(b16)
    dv = jnp.concatenate(dvs, axis=0).astype(b16)
    for c, m in enumerate((dq, dk, dv)):
        d_proj[c] = m
    d_proj.flush()
    a_v = a[...]
    grads = [dot(m, a_v) for m in (dq, dk, dv)]
    gain_rows = [
        jnp.sum(w[c].astype(f32) * grads[c], axis=0, keepdims=True) for c in range(3)
    ]
    gain_one = gain_rows[0] + gain_rows[1] + gain_rows[2]
    full = jnp.concatenate(grads + [g_out], axis=0)
    for l in range(6):
        cut = slice(128 * l, 128 * l + 128)
        scr[:, 24 * l : 24 * l + 24, :] = full[:, cut].reshape(NE, CAP, 128)
        scr[:, 144 + l, :] = router_t[:, cut]
    scr[:, 150:152, :] = jnp.zeros((NE, 2, 128), f32)
    for l in range(6):
        scr[l, 150:151, :] = gain_two[:, 128 * l : 128 * l + 128]
    wide = jnp.concatenate([bias, jnp.zeros((8, 96), f32)], axis=1)
    for h in range(NH):
        scr[6 + h, 150:151, :] = wide[h : h + 1]
    pay[...] = scr[...].astype(b16)
    gain_out[...] = gain_one


def input_grad_body(me, d_proj, w, gain, da0, da1, da2, da3, scr):
    scr[...] = dot(d_proj[0], w[0], TN) + dot(d_proj[1], w[1], TN) + dot(d_proj[2], w[2], TN)
    one = gain[...]
    hi = one.astype(b16).astype(f32)
    gl = jnp.concatenate([hi, one - hi, jnp.zeros((14, D), f32)], axis=0)
    for d, out in enumerate((da0, da1, da2, da3)):
        to = pl.multiple_of(lax.rem(me[0] + d, NS) * 128, 128)
        out[...] = jnp.concatenate([scr[pl.ds(to, 128), :], gl], axis=0).astype(b16)


def sum_body(me, held, pay, out):
    total = jnp.sum(pay[...].astype(f32), axis=0)
    gl = jnp.sum(jnp.sum(held[:, 128:, :].astype(f32), axis=0), axis=0, keepdims=True)
    gl = [gl[:, 128 * l : 128 * l + 128] for l in range(6)] + [jnp.zeros((2, 128), f32)]
    chunk = jnp.concatenate([total] + gl, axis=0).astype(b16)
    out[...] = jnp.broadcast_to(chunk[None], (NE, 160, 128))


def token_grad_body(me, gains, held, tok, dhid, out):
    d_a = jnp.sum(held[:, :128, :].astype(f32), axis=0)
    x = tok[...].astype(f32)
    r1 = inv_rms(x)
    n1 = x * r1
    v1 = d_a * gains[0:1, :]
    out[...] = (dhid[...] + r1 * (v1 - n1 * jnp.mean(v1 * n1, axis=-1, keepdims=True))).astype(b16)


def join_body(me, held, out):
    held.ready()
    out.flush(src=held.held)


def result_body(me, gate, held, hidden, out):
    value = unpack_rows([held[j] for j in range(NS)]).astype(f32)
    out[...] = (hidden[...] + gate[...] * value).astype(b16)


def finish_body(got, gains, qkv, proj, bias, gains_out, router, scr):
    scr[...] = got[...].astype(f32)
    full = jnp.concatenate([scr[:, 24 * l : 24 * l + 24, :].reshape(D, 128) for l in range(6)], axis=1)
    for c in range(3):
        qkv[c] = full[W * c : W * c + W]
        qkv.flush(c)
    proj[...] = full[3 * W :]
    router[...] = jnp.concatenate([scr[:, 144 + l, :] for l in range(6)], axis=1)
    gl = jnp.sum(scr[:, 152:160, :], axis=0)
    one = jnp.concatenate([gl[l : l + 1] for l in range(6)], axis=1) / gains[0:1, :]
    two = jnp.concatenate([scr[l, 150:151, :] for l in range(6)], axis=1)
    gains_out[...] = jnp.concatenate([one, two], axis=0)
    bias[...] = jnp.concatenate([scr[6 + h, 150:151, :NE] for h in range(NH)], axis=0)


def over_experts(v):
    return lax.all_to_all(v, "expert", split_axis=0, concat_axis=0, tiled=True)


def over_all(v):
    return lax.all_to_all(v, ("expert", "shard"), split_axis=0, concat_axis=0, tiled=True)


def rotate(v, d):
    return lax.ppermute(v, "shard", [(i, (i + d) % NS) for i in range(NS)])


def round_shard(v):
    return [v] + [rotate(v, d) for d in (1, 2, 3)]


def local(tokens, qkv_weight, out_proj, rel_bias, gains, router, w_in, w_out, route, slot, buckets, cotangent):
    w_in = w_in.reshape(D, -1)
    w_out = w_out.reshape(-1, D)
    ff = w_in.shape[1]
    me, expert = Place("shard"), Place("expert")
    route_row, slot_row = route[None, :], slot[None, :]
    bk = jnp.concatenate([jnp.flip(buckets), jnp.full((1,), -1, jnp.int32)])[None, :]
    w_t = jnp.transpose(qkv_weight, (0, 2, 1))
    router_t = router.T
    together = lax.optimization_barrier

    (g_rows,) = call(dispatch_body, [((NE, CAP, D), b16)], route_row, slot_row, cotangent, name="dispatch_cotangent")
    g_rows = over_experts(g_rows).reshape(SLOTS, D)
    w_pieces = round_shard(out_proj)
    heads, heads_t, a, qk_t, v, p = call(
        attend_body,
        [((D, 128), b16), ((W, T), b16), ((T, D), b16), ((2, W, T), b16), ((T, W), b16), ((NH, T, T), f32)],
        tokens, gains, Parts(w_t), rel_bias, bk, name="attend",
    )
    h_pieces = round_shard(heads)
    (w_full,) = call(order_weights_body, [((D, D), b16)], me, Pieces(w_pieces), name="order_weights", room=25)
    rows, u, hidden = call(
        mix_body,
        [((NE, CAP, D), b16), ((T, D), b16), ((T, D), f32)],
        me, route_row, slot_row, gains, Pieces(h_pieces), w_full, tokens, name="mix",
    )
    u_rows = over_experts(rows).reshape(SLOTS, D)
    (h,) = call(ungated_body, [((SLOTS, ff), f32)], g_rows, w_out, name="ungated")
    route_col, slot_col = route[:, None], slot[:, None]
    gate, coef = call(gate_body, [((T, 1), f32), ((T, NE), f32)], u, router_t, route_col, name="gate")
    u_rows, h, gate, coef, route_col, slot_col = together((u_rows, h, gate, coef, route_col, slot_col))
    ret, act, d_pre, row_gate = call(
        expert_body,
        [((NE, NS, 40, 128), b16), ((SLOTS, ff), b16), ((SLOTS, ff), b16), ((SLOTS, 1), f32)],
        expert, router_t, u_rows, w_in, h, name="expert",
    )
    back = over_all(ret.reshape(NE * NS, 40, 128)).reshape(NE, NS, 40, 128)
    (val,) = call(value_body, [((NE, NS, 40, 128), b16)], act, w_out, name="value")
    d_rows = (row_gate * g_rows.astype(f32)).astype(b16)
    grad_w_out = dot(act, d_rows, TN)
    grad_w_in = dot(u_rows, d_pre, TN)
    back, val, grad_w_out, grad_w_in = together((back, val, grad_w_out, grad_w_in))
    piece, d_gate = call(
        collect_body, [((D, 128), b16), ((T, 1), f32)], route_col, slot_col, back, name="collect_back"
    )
    b_pieces = round_shard(piece)
    value = over_all(val.reshape(NE * NS, 40, 128)).reshape(NE, NS, 40, 128)
    pay, d_proj, gain_one, d_hidden = call(
        backward_body,
        [((NE, PAY, 128), b16), ((3, W, T), b16), ((1, D), f32), ((T // NS, D), f32)],
        me, gains, d_gate, coef, router_t, Pieces(b_pieces), hidden, cotangent, out_proj, v, Parts(p), qk_t, heads_t, u,
        a, bk, w_t, name="backward", unheld=(3,),
        scratch=[pltpu.VMEM((NE, PAY, 128), f32), pltpu.VMEM((T, D), f32)],
    )
    pay, value, d_proj, gain_one = together((pay, value, d_proj, gain_one))
    pay = over_experts(pay)
    da = call(
        input_grad_body, [((144, D), b16)] * NS, me, d_proj, w_t, gain_one, name="input_grad",
        scratch=[pltpu.VMEM((T, D), f32)],
    )
    da = [da[0]] + [rotate(x, d) for d, x in enumerate(da) if d]
    (v_piece,) = call(collect_value_body, [((D, 128), b16)], route_col, slot_col, value, name="collect_value")
    v_pieces = round_shard(v_piece)
    (result,) = call(result_body, [((T, D), b16)], me, gate, Pieces(v_pieces), hidden, name="result", room=25)
    (chunk,) = call(sum_body, [((NE, 160, 128), b16)], me, Pieces(da), pay, name="sum_gradients", room=25)
    chunk = over_experts(chunk)
    (t_piece,) = call(
        token_grad_body, [((128, D), b16)], me, gains, Pieces(da), Quarter(tokens), d_hidden, name="token_grad", room=25,
    )
    t_pieces = round_shard(t_piece)
    (grad_tokens,) = call(join_body, [((NS, T // NS, D), b16)], me, Pieces(t_pieces), name="join_tokens", room=25, unheld=(0,))
    chunk, grad_tokens, result = together((chunk, grad_tokens, result))
    grad_qkv, grad_proj, grad_bias, grad_gains, grad_router = call(
        finish_body,
        [((3, W, D), f32), ((W, D), f32), ((NH, NE), f32), ((2, D), f32), ((NE, D), f32)],
        chunk, gains, name="finish", room=25, scratch=[pltpu.VMEM((NE, 160, 128), f32)],
    )
    grad_qkv = jnp.transpose(grad_qkv, (0, 2, 1))
    return (
        result, grad_tokens.reshape(T, D), grad_qkv, grad_proj, grad_bias, grad_gains, grad_router.T, grad_w_in[None],
        grad_w_out[None],
    )


def solution(mesh):
    in_specs = (
        P("expert", None),
        P(None, None, "shard"),
        P("shard", None),
        P("shard", None),
        P(),
        P(),
        P("expert", None, "shard"),
        P("expert", "shard", None),
        P("expert"),
        P("expert"),
        P(),
        P("expert", None),
    )
    out_specs = (
        P("expert", None),
        P("expert", None),
        P(None, None, "shard"),
        P("shard", None),
        P("shard", None),
        P(),
        P(),
        P("expert", None, "shard"),
        P("expert", "shard", None),
    )
    return jax.shard_map(local, mesh=mesh, in_specs=in_specs, out_specs=out_specs, check_vma=False)
```

```python
import jax
import jax.numpy as jnp
from jax import lax
from jax.experimental import pallas as pl
from jax.experimental.pallas import tpu as pltpu
from jax.sharding import PartitionSpec as P

EPS = 1e-06
T = 512
D = 768
NH = 3
HD = 64
W = NH * HD
NE = 32
CAP = 24
SLOTS = NE * CAP
NS = 4
SCALE = HD ** (-0.5)
f32 = jnp.float32
b16 = jnp.bfloat16

NN = (((1,), (0,)), ((), ()))
NT = (((1,), (1,)), ((), ()))
TN = (((0,), (0,)), ((), ()))


def dot(a, b, dims=NN):
    return lax.dot_general(a, b, dims, preferred_element_type=f32)


class Place:
    def __init__(self, axis):
        self.axis = axis


class Parts:
    def __init__(self, array):
        self.array = array


class Quarter:
    def __init__(self, array):
        self.array = array


class Pieces:
    def __init__(self, arrays, first=0, rows=None):
        self.arrays = arrays
        self.first, self.rows = first, arrays[0].shape[0] if rows is None else rows


class Hold:
    def __init__(self, array):
        self.array = array


class Load:
    def __init__(self, held, copies):
        self.held, self.copies = held, copies

    def start(self):
        for c in self.copies:
            c.start()

    def ready(self, at=None):
        for k, c in enumerate(self.copies):
            if c is not None and (at is None or at == k):
                c.wait()
                self.copies[k] = None

    def __getitem__(self, at):
        self.ready()
        return self.held[at]


class LoadParts(Load):
    def __getitem__(self, at):
        self.ready(at if isinstance(at, int) else at[0])
        return self.held[at]


class Store:
    def __init__(self, out, held, sems):
        self.out, self.held, self.sems, self.copies = out, held, sems, []

    def __setitem__(self, at, value):
        self.held[at] = value

    def flush(self, at=None, src=None):
        sem = self.sems.at[len(self.copies)]
        src = self.held if src is None else src
        if at is None:
            copy = pltpu.make_async_copy(src, self.out, sem)
        else:
            copy = pltpu.make_async_copy(src.at[at], self.out.at[at], sem)
        copy.start()
        self.copies.append(copy)

    def send(self, src, at):
        copy = pltpu.make_async_copy(src, self.out.at[at], self.sems.at[len(self.copies)])
        copy.start()
        self.copies.append(copy)

    def finish(self):
        for c in self.copies:
            c.wait()


def call(body, outs, *args, name, scratch=(), unheld=(), room=0):
    outs = [jax.ShapeDtypeStruct(s, t) for s, t in outs]
    hbm = pl.BlockSpec(memory_space=pltpu.HBM)
    flat, in_specs, buffers = [], [], []
    for a in args:
        if isinstance(a, Place):
            continue
        if isinstance(a, Pieces):
            flat += a.arrays
            in_specs += [hbm] * NS
            shape = (NS, a.rows) + a.arrays[0].shape[1:]
            buffers += [pltpu.VMEM(shape, a.arrays[0].dtype), pltpu.SemaphoreType.DMA((NS,))]
        elif isinstance(a, Parts):
            flat.append(a.array)
            in_specs.append(hbm)
            buffers += [pltpu.VMEM(a.array.shape, a.array.dtype), pltpu.SemaphoreType.DMA((a.array.shape[0],))]
        elif isinstance(a, Quarter):
            flat.append(a.array)
            in_specs.append(hbm)
            shape = (a.array.shape[0] // NS,) + a.array.shape[1:]
            buffers += [pltpu.VMEM(shape, a.array.dtype), pltpu.SemaphoreType.DMA((1,))]
        else:
            held = isinstance(a, Hold)
            flat.append(a.array if held else a)
            in_specs.append(hbm)
            buffers += [] if held else [pltpu.VMEM(a.shape, a.dtype), pltpu.SemaphoreType.DMA((1,))]
    for k, o in enumerate(outs):
        if k not in unheld:
            buffers.append(pltpu.VMEM(o.shape, o.dtype))
        buffers.append(pltpu.SemaphoreType.DMA((4,)))

    def kernel(*refs):
        ins = iter(refs[: len(flat)])
        results = refs[len(flat) : len(flat) + len(outs)]
        rest = refs[len(flat) + len(outs) :]
        bufs, user = iter(rest[: len(buffers)]), rest[len(buffers) :]
        given, me = [], None
        for a in args:
            if isinstance(a, Place):
                me = [lax.axis_index(a.axis)]
                given.append(me)
                continue
            if isinstance(a, Hold):
                given.append(next(ins))
                continue
            if isinstance(a, Pieces):
                held, sems = next(bufs), next(bufs)
                cut = pl.ds(a.first, a.rows)
                item = Load(held, [
                    pltpu.make_async_copy(next(ins).at[cut], held.at[lax.rem(me[0] + (NS - d), NS)], sems.at[d])
                    for d in range(NS)
                ])
            elif isinstance(a, Parts):
                ref, held, sems = next(ins), next(bufs), next(bufs)
                item = LoadParts(held, [
                    pltpu.make_async_copy(ref.at[k], held.at[k], sems.at[k]) for k in range(a.array.shape[0])
                ])
            elif isinstance(a, Quarter):
                ref, held, sems = next(ins), next(bufs), next(bufs)
                n = held.shape[0]
                at = pl.ds(pl.multiple_of(me[0] * n, n), n)
                item = Load(held, [pltpu.make_async_copy(ref.at[at], held, sems.at[0])])
            else:
                ref, held, sems = next(ins), next(bufs), next(bufs)
                item = Load(held, [pltpu.make_async_copy(ref, held, sems.at[0])])
            item.start()
            given.append(item)
        stores = []
        for k, out in enumerate(results):
            held = None if k in unheld else next(bufs)
            stores.append(Store(out, held, next(bufs)))
        body(*given, *stores, *user)
        for item in given:
            if isinstance(item, Load):
                item.ready()
        for item in stores:
            if not item.copies:
                item.flush()
        for item in stores:
            item.finish()

    return pl.pallas_call(
        kernel,
        out_shape=outs,
        in_specs=in_specs,
        out_specs=[hbm] * len(outs),
        scratch_shapes=buffers + list(scratch),
        compiler_params=pltpu.CompilerParams(vmem_limit_bytes=(60 - room) * 1024 * 1024),
        cost_estimate=pl.CostEstimate(flops=0, bytes_accessed=300000, transcendentals=0),
        name=name,
    )(*flat)


def lanes(shape):
    return lax.broadcasted_iota(jnp.int32, shape, len(shape) - 1)


def rows_of(shape):
    return lax.broadcasted_iota(jnp.int32, shape, len(shape) - 2)


def roll_half(v):
    return pltpu.roll(v, 64, v.ndim - 1)


def inv_rms(v):
    return lax.rsqrt(jnp.mean(v * v, axis=-1, keepdims=True) + EPS)


def toeplitz_rows(offsets_row, rows, shift):
    wide = jnp.broadcast_to(offsets_row, (rows, offsets_row.shape[1]))
    return pltpu.roll(wide, shift, 1, stride=1, stride_axis=0)


def bucket_hot(bk):
    return (bk == rows_of((NE, 1024))).astype(f32)


def pack_rows(block, half):
    low = lanes((T // 2, 128)) < 64
    tail = jnp.where(low, half[: T // 2], roll_half(half[T // 2 :]))
    return jnp.concatenate([block, tail], axis=0).astype(b16)


def unpack_rows(pieces):
    low = lanes((T // 2, 128)) < 64
    blocks = [p[:T] for p in pieces]
    for left, right in ((0, 1), (2, 3)):
        l_half = pieces[left][T:].astype(f32)
        r_half = pieces[right][T:].astype(f32)
        top = jnp.where(low, l_half, roll_half(r_half))
        bottom = jnp.where(low, roll_half(l_half), r_half)
        blocks.append(jnp.concatenate([top, bottom], axis=0).astype(b16))
    return jnp.concatenate(blocks, axis=1)


def dispatch_body(route, slot, val, out):
    hot = (route[...] * CAP + slot[...] == rows_of((SLOTS, T))).astype(b16)
    out[...] = dot(hot, val[...]).reshape(NE, CAP, D).astype(b16)


def attend_body(tok, gains, w, rb, bk, heads, heads_t, a_out, qk_t, v_out, p_out):
    x = tok[...].astype(f32)
    a = (x * inv_rms(x) * gains[0:1, :]).astype(b16)
    a_out[...] = a
    a_out.flush()
    q_t = dot(w[0], a, NT).astype(b16)
    v_t = dot(w[2], a, NT).astype(b16)
    k = dot(a, w[1], NT).astype(b16)
    qk_t[0] = q_t
    qk_t[1] = dot(w[1], a, NT).astype(b16)
    qk_t.flush()
    v_out[...] = dot(a, w[2], NT).astype(b16)
    v_out.flush()
    off = lax.dot_general(rb[...], bucket_hot(bk[...]), NN, precision=lax.Precision.HIGHEST, preferred_element_type=f32)
    outs = []
    for h in range(NH):
        part = slice(HD * h, HD * h + HD)
        s = dot(k[:, part], q_t[part]) * SCALE
        wide = toeplitz_rows(off[h : h + 1], 128, 897)
        bias = jnp.concatenate([wide[:, 384 - 128 * b : 896 - 128 * b] for b in range(4)], axis=0)
        s = s + bias
        e = jnp.exp(s - jnp.max(s, axis=0, keepdims=True))
        p = e / jnp.sum(e, axis=0, keepdims=True)
        p_out[h] = p
        p_out.flush(h)
        outs.append(dot(v_t[part], p.astype(b16)))
    heads_t[...] = jnp.concatenate(outs, axis=0).astype(b16)
    block = jnp.concatenate(outs[:2], axis=0).T
    tail = jnp.concatenate([outs[2][:, : T // 2], outs[2][:, T // 2 :]], axis=0).T
    heads[...] = jnp.concatenate([block, tail], axis=0).astype(b16)


def order_weights_body(me, held, out):
    parts = [held[j, :128] for j in range(NS)] + [held[j, 128:] for j in range(NS)]
    out[...] = jnp.concatenate(parts, axis=0)


def mix_body(me, route, slot, gains, held, w, tok, rows, u_out, hidden_out):
    full = unpack_rows([held[j] for j in range(NS)])
    hidden = tok[...].astype(f32) + dot(full, w[...])
    u = (hidden * inv_rms(hidden) * gains[1:2, :]).astype(b16)
    hidden_out[...] = hidden
    hidden_out.flush()
    u_out[...] = u
    u_out.flush()
    hot = (route[...] * CAP + slot[...] == rows_of((SLOTS, T))).astype(b16)
    rows[...] = dot(hot, u).reshape(NE, CAP, D).astype(b16)


def gate_body(u, router, route, slot, gate_out, coef_out, index_out):
    index_out[...] = route[...] * CAP + slot[...]
    logits = dot(u[...], router[...], NT)
    e = jnp.exp(logits - jnp.max(logits, axis=1, keepdims=True))
    probs = e / jnp.sum(e, axis=1, keepdims=True)
    chosen = (route[...] == lanes((T, NE))).astype(f32)
    gate = jnp.sum(probs * chosen, axis=1, keepdims=True)
    coef = probs * (chosen - gate)
    gate_out[...] = gate
    coef_out[...] = coef


def ungated_body(g, w_out, h):
    h[...] = dot(g[...], w_out[...], NT)


def pack_return(val, extra=None):
    n = val.shape[0] // CAP
    low = lanes((n, 8, 128)) < 64
    if extra is not None:
        ext = extra.reshape(n, CAP, 1)
        hi = ext.astype(b16).astype(f32)
        lo = ext - hi
        lane = lanes((n, 8, 128))
        tail = jnp.zeros((n, 8, 128), f32)
        for t in range(3):
            tail = jnp.where(lane == 64 + t, hi[:, 8 * t : 8 * t + 8], tail)
            tail = jnp.where(lane == 67 + t, lo[:, 8 * t : 8 * t + 8], tail)
    else:
        tail = jnp.zeros((n, 8, 128), f32)
    res = []
    for s in range(NS):
        block = val[:, 128 * s : 128 * s + 128].reshape(n, CAP, 128)
        c = 512 + 128 * (s // 2)
        half = val[:, c : c + 128].reshape(n, CAP, 128)
        moved = roll_half(half)
        x0, x1, x2 = (half[:, 8 * t : 8 * t + 8] for t in range(3))
        r0, r1, r2 = (moved[:, 8 * t : 8 * t + 8] for t in range(3))
        if s % 2 == 0:
            t3, t4 = jnp.where(low, x0, r1), jnp.where(low, x2, tail)
        else:
            t3, t4 = jnp.where(low, r0, x1), jnp.where(low, r2, tail)
        res.append(jnp.concatenate([block, t3, t4], axis=1))
    return [r.astype(b16) for r in res]


MAIN = 144
PAY = 160

GELU_C = 0.7978845608028654


def expert_body(me, router, rows, w_in, h, ret, act_out, dpre_out, gate_out):
    half = SLOTS // 2
    for i in range(2):
        cut = slice(half * i, half * i + half)
        seqs = slice(NE // 2 * i, NE // 2 * (i + 1))
        u = rows[cut, :]
        logits = dot(u, router[...], NT)
        e = jnp.exp(logits - jnp.max(logits, axis=1, keepdims=True))
        mine = (lanes(logits.shape) == me[0]).astype(f32)
        gate = jnp.sum(e * mine, axis=1, keepdims=True) / jnp.sum(e, axis=1, keepdims=True)
        pre = dot(u, w_in[...])
        sq = pre * pre
        th = jnp.tanh(GELU_C * pre * (1.0 + 0.044715 * sq))
        act = (0.5 * pre * (1.0 + th)).astype(b16)
        slope = 0.5 * (1.0 + th) + 0.5 * pre * (1.0 - th * th) * (GELU_C * (1.0 + 3 * 0.044715 * sq))
        hv = h[cut, :]
        d_gate = jnp.sum(act.astype(f32) * hv, axis=1, keepdims=True)
        d_pre = (gate * hv * slope).astype(b16)
        grads = pack_return(dot(d_pre, w_in[...], NT), d_gate)
        for s in range(NS):
            ret[seqs, s] = grads[s]
        ret.flush(seqs)
        act_out[cut, :] = act
        dpre_out[cut, :] = d_pre
        gate_out[cut, :] = gate


def value_body(act, w_out, out):
    out[...] = dot(act[...], w_out[...]).reshape(NE, CAP, D).astype(b16)


def unpack_return(total):
    block = total[:, :CAP].reshape(SLOTS, 128).astype(b16)
    t3 = total[:, 24:32]
    t4 = total[:, 32:40]
    return block, jnp.concatenate([t3, roll_half(t3), t4], axis=1).reshape(SLOTS, 128), t4


def collect_body(index, got, piece, d_gate):
    block, half, t4 = unpack_return(jnp.sum(got[...].astype(f32), axis=1))
    lane = lanes((SLOTS, 128))
    tl = lanes(t4.shape)
    cols = []
    for t in range(3):
        cols.append(jnp.sum(jnp.where((tl == 64 + t) | (tl == 67 + t), t4, 0.0), axis=2, keepdims=True))
    col = jnp.concatenate(cols, axis=1).reshape(SLOTS, 1)
    hi = col.astype(b16).astype(f32)
    half = jnp.where(lane < 64, half, jnp.where(lane == 64, hi, jnp.where(lane == 65, col - hi, 0.0)))
    hot = (index[...] == lanes((T, SLOTS))).astype(b16)
    mine = dot(hot, jnp.concatenate([block, half.astype(b16)], axis=1))
    piece[...] = pack_rows(mine[:, :128], mine[:, 128:])
    piece.flush()
    lt = lanes((T, 128))
    d_gate[...] = jnp.sum(jnp.where((lt == 64) | (lt == 65), mine[:, 128:], 0.0), axis=1, keepdims=True)


def backward_body(
    me, gains, d_gate, coef, router, held, hidden_in, cot, out_proj, v, p, qk_t, heads_t, u, a, bk, w,
    pay, d_proj, gain_out, dhid_out, scr, dhid,
):
    d_expert = unpack_rows([held[j] for j in range(NS)]).astype(f32)
    dg = d_gate[...]
    d_logits = coef[...] * dg
    high = d_logits.astype(b16)
    low = (d_logits - high.astype(f32)).astype(b16)
    d_u = dot(high, router[...]) + dot(low, router[...]) + d_expert
    hidden = hidden_in[...]
    r2 = inv_rms(hidden)
    n2 = hidden * r2
    gain_two = jnp.sum(d_u * n2, axis=0, keepdims=True)
    v2 = d_u * gains[1:2, :]
    d_hidden = cot[...].astype(f32) + r2 * (v2 - n2 * jnp.mean(v2 * n2, axis=-1, keepdims=True))
    dhid[...] = d_hidden
    dhid_out.flush(src=dhid.at[pl.ds(pl.multiple_of(me[0] * 128, 128), 128)])
    d_att = d_hidden.astype(b16)
    router_t = dot(high, u[...], TN) + dot(low, u[...], TN)
    g_out = dot(heads_t[...], d_att)
    do_t = dot(out_proj[...], d_att, NT).astype(b16)
    hot = bucket_hot(bk[...])
    dqs, dks, dvs, bias = [], [], [], []
    for h in range(NH):
        part = slice(HD * h, HD * h + HD)
        prob = p[h]
        dp = dot(v[:, part], do_t[part])
        delta = jnp.sum(prob * dp, axis=0, keepdims=True)
        ds = (prob * (dp - delta)).astype(b16)
        dvs.append(dot(do_t[part], prob.astype(b16), NT))
        dks.append(dot(qk_t[0, part], ds, NT) * SCALE)
        dqs.append(dot(qk_t[1, part], ds) * SCALE)
        ds_f = ds.astype(f32)
        acc = jnp.zeros((128, 1024), f32)
        for b in range(4):
            left, right = 384 - 128 * b, 128 + 128 * b
            blk = ds_f[128 * b : 128 * b + 128]
            parts = ([jnp.zeros((128, left), f32)] if left else []) + [blk, jnp.zeros((128, right), f32)]
            acc = acc + jnp.concatenate(parts, axis=1)
        for step in (64, 32, 16, 8):
            acc = acc[:step] + pltpu.roll(acc[step:], 1024 - step, 1)
        row = rows_of((8, 1024))
        for step in (4, 2, 1):
            acc = jnp.where((row & step) != 0, pltpu.roll(acc, 1024 - step, 1), acc)
        bias.append(pltpu.roll(jnp.sum(acc, axis=0, keepdims=True), 127, 1))
    bias = lax.dot_general(
        jnp.concatenate(bias + [jnp.zeros((5, 1024), f32)], axis=0), hot, NT,
        precision=lax.Precision.HIGHEST, preferred_element_type=f32,
    )
    dq = jnp.concatenate(dqs, axis=0).astype(b16)
    dk = jnp.concatenate(dks, axis=0).astype(b16)
    dv = jnp.concatenate(dvs, axis=0).astype(b16)
    for c, m in enumerate((dq, dk, dv)):
        d_proj[c] = m
    d_proj.flush()
    a_v = a[...]
    grads = [dot(m, a_v) for m in (dq, dk, dv)]
    gain_rows = [
        jnp.sum(w[c].astype(f32) * grads[c], axis=0, keepdims=True) for c in range(3)
    ]
    gain_one = gain_rows[0] + gain_rows[1] + gain_rows[2]
    full = jnp.concatenate([g.astype(b16) for g in grads + [g_out]], axis=0)
    big = jnp.concatenate([full[:, 128 * l : 128 * l + 128] for l in range(6)], axis=0)
    for c in range(NE):
        pay[c, :MAIN] = big[MAIN * c : MAIN * c + MAIN]
    scr[:, 6:, :] = jnp.zeros((NE, 10, 128), f32)
    wide = jnp.concatenate([bias, jnp.zeros((8, 96), f32)], axis=1)
    for l in range(6):
        scr[:, l, :] = router_t[:, 128 * l : 128 * l + 128]
        scr[l, 6:7, :] = gain_two[:, 128 * l : 128 * l + 128]
    for h in range(NH):
        scr[6 + h, 6:7, :] = wide[h : h + 1]
    pay[:, MAIN:, :] = scr[...].astype(b16)
    gain_out[...] = gain_one


def input_grad_body(me, gain, index, got, d_proj, w, da0, da1, da2, da3, grads, values):
    hot = (index[...] == lanes((T, SLOTS))).astype(b16)
    values[...] = dot(hot, got[...])
    grads[...] = dot(d_proj[0], w[0], TN) + dot(d_proj[1], w[1], TN) + dot(d_proj[2], w[2], TN)
    one = gain[...]
    hi = one.astype(b16).astype(f32)
    gl = jnp.concatenate([hi, one - hi, jnp.zeros((14, D), f32)], axis=0).astype(b16)
    for d, out in enumerate((da0, da1, da2, da3)):
        to = pl.ds(pl.multiple_of(lax.rem(me[0] + d, NS) * 128, 128), 128)
        out[:128] = grads[to, :].astype(b16)
        out[128:144] = gl
        out[144:] = values[to, :].astype(b16)
        out.flush()


def sum_body(me, held, pay, out):
    total = jnp.sum(pay[...].astype(f32), axis=0)
    gl = jnp.sum(jnp.sum(held[...].astype(f32), axis=0), axis=0, keepdims=True)
    gl = [gl[:, 128 * l : 128 * l + 128] for l in range(6)] + [jnp.zeros((2, 128), f32)]
    chunk = jnp.concatenate([total[: MAIN + 8]] + gl, axis=0).astype(b16)
    out[...] = jnp.broadcast_to(chunk[None], (NE, PAY, 128))


def token_grad_body(me, gains, held, tok, dhid, gate, hidden, out):
    d_a = jnp.sum(held[:, :128, :].astype(f32), axis=0)
    x = tok[...].astype(f32)
    r1 = inv_rms(x)
    n1 = x * r1
    v1 = d_a * gains[0:1, :]
    grad = dhid[...] + r1 * (v1 - n1 * jnp.mean(v1 * n1, axis=-1, keepdims=True))
    value = jnp.sum(held[:, 144:, :].astype(f32), axis=0).astype(b16).astype(f32)
    out[:128] = (hidden[...] + gate[...] * value).astype(b16)
    out[128:] = grad.astype(b16)


def tokens_body(me, held, result, grad):
    held.ready()
    for j in range(NS):
        rows = pl.ds(128 * j, 128)
        result.send(held.held.at[j, pl.ds(0, 128)], rows)
        grad.send(held.held.at[j, pl.ds(128, 128)], rows)


def finish_body(got, gains, qkv, proj, bias, gains_out, router, scr):
    big = jnp.concatenate([got[c, :MAIN] for c in range(NE)], axis=0)
    full = jnp.concatenate([big[D * l : D * l + D] for l in range(6)], axis=1)
    for c in range(3):
        qkv[c] = full[W * c : W * c + W].astype(f32)
        qkv.flush(c)
    proj[...] = full[3 * W :].astype(f32)
    proj.flush()
    scr[...] = got[:, MAIN:, :].astype(f32)
    router[...] = jnp.concatenate([scr[:, l, :] for l in range(6)], axis=1)
    gl = jnp.sum(scr[:, 8:, :], axis=0)
    one = jnp.concatenate([gl[l : l + 1] for l in range(6)], axis=1) / gains[0:1, :]
    two = jnp.concatenate([scr[l, 6:7, :] for l in range(6)], axis=1)
    gains_out[...] = jnp.concatenate([one, two], axis=0)
    bias[...] = jnp.concatenate([scr[6 + h, 6:7, :NE] for h in range(NH)], axis=0)


def over_experts(v):
    return lax.all_to_all(v, "expert", split_axis=0, concat_axis=0, tiled=True)


def over_all(v):
    return lax.all_to_all(v, ("expert", "shard"), split_axis=0, concat_axis=0, tiled=True)


def rotate(v, d):
    return lax.ppermute(v, "shard", [(i, (i + d) % NS) for i in range(NS)])


def round_shard(v):
    return [v] + [rotate(v, d) for d in (1, 2, 3)]


def local(tokens, qkv_weight, out_proj, rel_bias, gains, router, w_in, w_out, route, slot, buckets, cotangent):
    w_in = w_in.reshape(D, -1)
    w_out = w_out.reshape(-1, D)
    ff = w_in.shape[1]
    me, expert = Place("shard"), Place("expert")
    route_row, slot_row = route[None, :], slot[None, :]
    bk = jnp.concatenate([jnp.flip(buckets), jnp.full((1,), -1, jnp.int32)])[None, :]
    w_t = jnp.transpose(qkv_weight, (0, 2, 1))
    router_t = router.T
    together = lax.optimization_barrier

    (g_rows,) = call(dispatch_body, [((NE, CAP, D), b16)], route_row, slot_row, cotangent, name="dispatch_cotangent")
    g_rows = over_experts(g_rows).reshape(SLOTS, D)
    w_pieces = round_shard(out_proj)
    heads, heads_t, a, qk_t, v, p = call(
        attend_body,
        [((D, 128), b16), ((W, T), b16), ((T, D), b16), ((2, W, T), b16), ((T, W), b16), ((NH, T, T), f32)],
        tokens, gains, Parts(w_t), rel_bias, bk, name="attend",
    )
    h_pieces = round_shard(heads)
    (w_full,) = call(order_weights_body, [((D, D), b16)], me, Pieces(w_pieces), name="order_weights", room=25)
    rows, u, hidden = call(
        mix_body,
        [((NE, CAP, D), b16), ((T, D), b16), ((T, D), f32)],
        me, route_row, slot_row, gains, Pieces(h_pieces), w_full, tokens, name="mix",
    )
    u_rows = over_experts(rows).reshape(SLOTS, D)
    (h,) = call(ungated_body, [((SLOTS, ff), f32)], g_rows, w_out, name="ungated")
    gate, coef, index = call(
        gate_body, [((T, 1), f32), ((T, NE), f32), ((T, 1), jnp.int32)], u, router_t, route[:, None], slot[:, None],
        name="gate",
    )
    u_rows, h, gate, coef, index = together((u_rows, h, gate, coef, index))
    ret, act, d_pre, row_gate = call(
        expert_body,
        [((NE, NS, 40, 128), b16), ((SLOTS, ff), b16), ((SLOTS, ff), b16), ((SLOTS, 1), f32)],
        expert, router_t, u_rows, w_in, h, name="expert",
    )
    back = over_all(ret.reshape(NE * NS, 40, 128)).reshape(NE, NS, 40, 128)
    (val,) = call(value_body, [((NE, CAP, D), b16)], act, w_out, name="value")
    d_rows = (row_gate * g_rows.astype(f32)).astype(b16)
    grad_w_out = dot(act, d_rows, TN)
    grad_w_in = dot(u_rows, d_pre, TN)
    back, val, grad_w_out, grad_w_in = together((back, val, grad_w_out, grad_w_in))
    piece, d_gate = call(
        collect_body, [((D, 128), b16), ((T, 1), f32)], index, back, name="collect_back", room=25
    )
    b_pieces = round_shard(piece)
    value = over_experts(val).reshape(SLOTS, D)
    pay, d_proj, gain_one, d_hidden = call(
        backward_body,
        [((NE, PAY, 128), b16), ((3, W, T), b16), ((1, D), f32), ((T // NS, D), f32)],
        me, gains, d_gate, coef, router_t, Pieces(b_pieces), hidden, cotangent, out_proj, v, Parts(p), qk_t, heads_t, u,
        a, bk, w_t, name="backward", unheld=(3,),
        scratch=[pltpu.VMEM((NE, 16, 128), f32), pltpu.VMEM((T, D), f32)],
    )
    pay, value, d_proj, gain_one = together((pay, value, d_proj, gain_one))
    pay = over_experts(pay)
    da = call(
        input_grad_body, [((272, D), b16)] * NS, me, gain_one, index, value, d_proj, w_t, name="input_grad",
        scratch=[pltpu.VMEM((T, D), f32), pltpu.VMEM((T, D), f32)],
    )
    da = [da[0]] + [rotate(x, d) for d, x in enumerate(da) if d]
    (t_piece,) = call(
        token_grad_body, [((256, D), b16)], me, gains, Pieces(da), Quarter(tokens), d_hidden,
        Quarter(gate), Quarter(hidden), name="token_grad",
    )
    (chunk,) = call(sum_body, [((NE, PAY, 128), b16)], me, Pieces(da, 128, 16), pay, name="sum_gradients", room=25)
    chunk = over_experts(chunk)
    result, grad_tokens = call(
        tokens_body, [((T, D), b16), ((T, D), b16)], me, Pieces(round_shard(t_piece)), name="tokens", room=25,
        unheld=(0, 1),
    )
    chunk, grad_tokens, result = together((chunk, grad_tokens, result))
    grad_qkv, grad_proj, grad_bias, grad_gains, grad_router = call(
        finish_body,
        [((3, W, D), f32), ((W, D), f32), ((NH, NE), f32), ((2, D), f32), ((NE, D), f32)],
        chunk, gains, name="finish", room=25, scratch=[pltpu.VMEM((NE, 16, 128), f32)],
    )
    grad_qkv = jnp.transpose(grad_qkv, (0, 2, 1))
    return (
        result, grad_tokens, grad_qkv, grad_proj, grad_bias, grad_gains, grad_router.T, grad_w_in[None],
        grad_w_out[None],
    )


def solution(mesh):
    in_specs = (
        P("expert", None),
        P(None, None, "shard"),
        P("shard", None),
        P("shard", None),
        P(),
        P(),
        P("expert", None, "shard"),
        P("expert", "shard", None),
        P("expert"),
        P("expert"),
        P(),
        P("expert", None),
    )
    out_specs = (
        P("expert", None),
        P("expert", None),
        P(None, None, "shard"),
        P("shard", None),
        P("shard", None),
        P(),
        P(),
        P("expert", None, "shard"),
        P("expert", "shard", None),
    )
    return jax.shard_map(local, mesh=mesh, in_specs=in_specs, out_specs=out_specs, check_vma=False)
```

```python
import jax
import jax.numpy as jnp
from jax import lax
from jax.experimental import pallas as pl
from jax.experimental.pallas import tpu as pltpu
from jax.sharding import PartitionSpec as P

EPS = 1e-06
T = 512
D = 768
NH = 3
HD = 64
W = NH * HD
NE = 32
CAP = 24
SLOTS = NE * CAP
NS = 4
SCALE = HD ** (-0.5)
f32 = jnp.float32
b16 = jnp.bfloat16

NN = (((1,), (0,)), ((), ()))
NT = (((1,), (1,)), ((), ()))
TN = (((0,), (0,)), ((), ()))


def dot(a, b, dims=NN):
    return lax.dot_general(a, b, dims, preferred_element_type=f32)


class Place:
    def __init__(self, axis):
        self.axis = axis


class Parts:
    def __init__(self, array):
        self.array = array


class Quarter:
    def __init__(self, array):
        self.array = array


class Pieces:
    def __init__(self, arrays, first=0, rows=None):
        self.arrays = arrays
        self.first = first if isinstance(first, tuple) else (first,) * NS
        self.rows = arrays[0].shape[0] if rows is None else rows


class Hold:
    def __init__(self, array):
        self.array = array


class Load:
    def __init__(self, held, copies):
        self.held, self.copies = held, copies

    def start(self):
        for c in self.copies:
            c.start()

    def ready(self, at=None):
        for k, c in enumerate(self.copies):
            if c is not None and (at is None or at == k):
                c.wait()
                self.copies[k] = None

    def __getitem__(self, at):
        self.ready()
        return self.held[at]


class LoadParts(Load):
    def __getitem__(self, at):
        self.ready(at if isinstance(at, int) else at[0])
        return self.held[at]


class Store:
    def __init__(self, out, held, sems):
        self.out, self.held, self.sems, self.copies = out, held, sems, []

    def __setitem__(self, at, value):
        self.held[at] = value

    def flush(self, at=None, src=None):
        sem = self.sems.at[len(self.copies)]
        src = self.held if src is None else src
        if at is None:
            copy = pltpu.make_async_copy(src, self.out, sem)
        else:
            copy = pltpu.make_async_copy(src.at[at], self.out.at[at], sem)
        copy.start()
        self.copies.append(copy)

    def send(self, src, at):
        copy = pltpu.make_async_copy(src, self.out.at[at], self.sems.at[len(self.copies)])
        copy.start()
        self.copies.append(copy)

    def finish(self):
        for c in self.copies:
            c.wait()


def call(body, outs, *args, name, scratch=(), unheld=(), room=0):
    outs = [jax.ShapeDtypeStruct(s, t) for s, t in outs]
    hbm = pl.BlockSpec(memory_space=pltpu.HBM)
    flat, in_specs, buffers = [], [], []
    for a in args:
        if isinstance(a, Place):
            continue
        if isinstance(a, Pieces):
            flat += a.arrays
            in_specs += [hbm] * NS
            shape = (NS, a.rows) + a.arrays[0].shape[1:]
            buffers += [pltpu.VMEM(shape, a.arrays[0].dtype), pltpu.SemaphoreType.DMA((NS,))]
        elif isinstance(a, Parts):
            flat.append(a.array)
            in_specs.append(hbm)
            buffers += [pltpu.VMEM(a.array.shape, a.array.dtype), pltpu.SemaphoreType.DMA((a.array.shape[0],))]
        elif isinstance(a, Quarter):
            flat.append(a.array)
            in_specs.append(hbm)
            shape = (a.array.shape[0] // NS,) + a.array.shape[1:]
            buffers += [pltpu.VMEM(shape, a.array.dtype), pltpu.SemaphoreType.DMA((1,))]
        else:
            held = isinstance(a, Hold)
            flat.append(a.array if held else a)
            in_specs.append(hbm)
            buffers += [] if held else [pltpu.VMEM(a.shape, a.dtype), pltpu.SemaphoreType.DMA((1,))]
    for k, o in enumerate(outs):
        if k not in unheld:
            buffers.append(pltpu.VMEM(o.shape, o.dtype))
        buffers.append(pltpu.SemaphoreType.DMA((4,)))

    def kernel(*refs):
        ins = iter(refs[: len(flat)])
        results = refs[len(flat) : len(flat) + len(outs)]
        rest = refs[len(flat) + len(outs) :]
        bufs, user = iter(rest[: len(buffers)]), rest[len(buffers) :]
        given, me = [], None
        for a in args:
            if isinstance(a, Place):
                me = [lax.axis_index(a.axis)]
                given.append(me)
                continue
            if isinstance(a, Hold):
                given.append(next(ins))
                continue
            if isinstance(a, Pieces):
                held, sems = next(bufs), next(bufs)
                item = Load(held, [
                    pltpu.make_async_copy(next(ins).at[pl.ds(a.first[d], a.rows)], held.at[lax.rem(me[0] + (NS - d), NS)], sems.at[d])
                    for d in range(NS)
                ])
            elif isinstance(a, Parts):
                ref, held, sems = next(ins), next(bufs), next(bufs)
                item = LoadParts(held, [
                    pltpu.make_async_copy(ref.at[k], held.at[k], sems.at[k]) for k in range(a.array.shape[0])
                ])
            elif isinstance(a, Quarter):
                ref, held, sems = next(ins), next(bufs), next(bufs)
                n = held.shape[0]
                at = pl.ds(pl.multiple_of(me[0] * n, n), n)
                item = Load(held, [pltpu.make_async_copy(ref.at[at], held, sems.at[0])])
            else:
                ref, held, sems = next(ins), next(bufs), next(bufs)
                item = Load(held, [pltpu.make_async_copy(ref, held, sems.at[0])])
            item.start()
            given.append(item)
        stores = []
        for k, out in enumerate(results):
            held = None if k in unheld else next(bufs)
            stores.append(Store(out, held, next(bufs)))
        body(*given, *stores, *user)
        for item in given:
            if isinstance(item, Load):
                item.ready()
        for item in stores:
            if not item.copies:
                item.flush()
        for item in stores:
            item.finish()

    return pl.pallas_call(
        kernel,
        out_shape=outs,
        in_specs=in_specs,
        out_specs=[hbm] * len(outs),
        scratch_shapes=buffers + list(scratch),
        compiler_params=pltpu.CompilerParams(vmem_limit_bytes=(60 - room) * 1024 * 1024),
        cost_estimate=pl.CostEstimate(flops=0, bytes_accessed=300000, transcendentals=0),
        name=name,
    )(*flat)


def lanes(shape):
    return lax.broadcasted_iota(jnp.int32, shape, len(shape) - 1)


def rows_of(shape):
    return lax.broadcasted_iota(jnp.int32, shape, len(shape) - 2)


def roll_half(v):
    return pltpu.roll(v, 64, v.ndim - 1)


def inv_rms(v):
    return lax.rsqrt(jnp.mean(v * v, axis=-1, keepdims=True) + EPS)


def toeplitz_rows(offsets_row, rows, shift):
    wide = jnp.broadcast_to(offsets_row, (rows, offsets_row.shape[1]))
    return pltpu.roll(wide, shift, 1, stride=1, stride_axis=0)


def bucket_hot(bk):
    return (bk == rows_of((NE, 1024))).astype(f32)


def pack_rows(block, half):
    low = lanes((T // 2, 128)) < 64
    tail = jnp.where(low, half[: T // 2], roll_half(half[T // 2 :]))
    return jnp.concatenate([block, tail], axis=0).astype(b16)


def unpack_rows(pieces):
    low = lanes((T // 2, 128)) < 64
    blocks = [p[:T] for p in pieces]
    for left, right in ((0, 1), (2, 3)):
        l_half = pieces[left][T:].astype(f32)
        r_half = pieces[right][T:].astype(f32)
        top = jnp.where(low, l_half, roll_half(r_half))
        bottom = jnp.where(low, roll_half(l_half), r_half)
        blocks.append(jnp.concatenate([top, bottom], axis=0).astype(b16))
    return jnp.concatenate(blocks, axis=1)


def dispatch_body(route, slot, val, out):
    hot = (route[...] * CAP + slot[...] == rows_of((SLOTS, T))).astype(b16)
    out[...] = dot(hot, val[...]).reshape(NE, CAP, D).astype(b16)


def attend_body(tok, gains, w, rb, bk, heads, heads_t, a_out, qk_t, v_out, p_out):
    x = tok[...].astype(f32)
    a = (x * inv_rms(x) * gains[0:1, :]).astype(b16)
    a_out[...] = a
    a_out.flush()
    q_t = dot(w[0], a, NT).astype(b16)
    v_t = dot(w[2], a, NT).astype(b16)
    k = dot(a, w[1], NT).astype(b16)
    qk_t[0] = q_t
    qk_t[1] = dot(w[1], a, NT).astype(b16)
    qk_t.flush()
    v_out[...] = dot(a, w[2], NT).astype(b16)
    v_out.flush()
    off = lax.dot_general(rb[...], bucket_hot(bk[...]), NN, precision=lax.Precision.HIGHEST, preferred_element_type=f32)
    outs = []
    for h in range(NH):
        part = slice(HD * h, HD * h + HD)
        s = dot(k[:, part], q_t[part]) * SCALE
        wide = toeplitz_rows(off[h : h + 1], 128, 897)
        bias = jnp.concatenate([wide[:, 384 - 128 * b : 896 - 128 * b] for b in range(4)], axis=0)
        s = s + bias
        e = jnp.exp(s - jnp.max(s, axis=0, keepdims=True))
        p = e / jnp.sum(e, axis=0, keepdims=True)
        p_out[h] = p
        p_out.flush(h)
        outs.append(dot(v_t[part], p.astype(b16)))
    heads_t[...] = jnp.concatenate(outs, axis=0).astype(b16)
    block = jnp.concatenate(outs[:2], axis=0).T
    tail = jnp.concatenate([outs[2][:, : T // 2], outs[2][:, T // 2 :]], axis=0).T
    heads[...] = jnp.concatenate([block, tail], axis=0).astype(b16)


def order_weights_body(me, held, out):
    parts = [held[j, :128] for j in range(NS)] + [held[j, 128:] for j in range(NS)]
    out[...] = jnp.concatenate(parts, axis=0)


def mix_body(me, route, slot, gains, held, w, tok, rows, u_out, hidden_out):
    full = unpack_rows([held[j] for j in range(NS)])
    hidden = tok[...].astype(f32) + dot(full, w[...])
    u = (hidden * inv_rms(hidden) * gains[1:2, :]).astype(b16)
    hidden_out[...] = hidden
    hidden_out.flush()
    u_out[...] = u
    u_out.flush()
    hot = (route[...] * CAP + slot[...] == rows_of((SLOTS, T))).astype(b16)
    rows[...] = dot(hot, u).reshape(NE, CAP, D).astype(b16)


def gate_body(u, router, route, slot, gate_out, coef_out, index_out):
    index_out[...] = route[...] * CAP + slot[...]
    logits = dot(u[...], router[...], NT)
    e = jnp.exp(logits - jnp.max(logits, axis=1, keepdims=True))
    probs = e / jnp.sum(e, axis=1, keepdims=True)
    chosen = (route[...] == lanes((T, NE))).astype(f32)
    gate = jnp.sum(probs * chosen, axis=1, keepdims=True)
    coef = probs * (chosen - gate)
    gate_out[...] = gate
    coef_out[...] = coef


def ungated_body(g, w_out, h):
    h[...] = dot(g[...], w_out[...], NT)


def pack_return(val, extra=None):
    n = val.shape[0] // CAP
    low = lanes((n, 8, 128)) < 64
    if extra is not None:
        ext = extra.reshape(n, CAP, 1)
        hi = ext.astype(b16).astype(f32)
        lo = ext - hi
        lane = lanes((n, 8, 128))
        tail = jnp.zeros((n, 8, 128), f32)
        for t in range(3):
            tail = jnp.where(lane == 64 + t, hi[:, 8 * t : 8 * t + 8], tail)
            tail = jnp.where(lane == 67 + t, lo[:, 8 * t : 8 * t + 8], tail)
    else:
        tail = jnp.zeros((n, 8, 128), f32)
    res = []
    for s in range(NS):
        block = val[:, 128 * s : 128 * s + 128].reshape(n, CAP, 128)
        c = 512 + 128 * (s // 2)
        half = val[:, c : c + 128].reshape(n, CAP, 128)
        moved = roll_half(half)
        x0, x1, x2 = (half[:, 8 * t : 8 * t + 8] for t in range(3))
        r0, r1, r2 = (moved[:, 8 * t : 8 * t + 8] for t in range(3))
        if s % 2 == 0:
            t3, t4 = jnp.where(low, x0, r1), jnp.where(low, x2, tail)
        else:
            t3, t4 = jnp.where(low, r0, x1), jnp.where(low, r2, tail)
        res.append(jnp.concatenate([block, t3, t4], axis=1))
    return [r.astype(b16) for r in res]


MAIN = 144
PAY = 160

GELU_C = 0.7978845608028654


def expert_body(me, router, rows, w_in, h, ret, act_out, dpre_out, gate_out):
    half = SLOTS // 2
    for i in range(2):
        cut = slice(half * i, half * i + half)
        seqs = slice(NE // 2 * i, NE // 2 * (i + 1))
        u = rows[cut, :]
        logits = dot(u, router[...], NT)
        e = jnp.exp(logits - jnp.max(logits, axis=1, keepdims=True))
        mine = (lanes(logits.shape) == me[0]).astype(f32)
        gate = jnp.sum(e * mine, axis=1, keepdims=True) / jnp.sum(e, axis=1, keepdims=True)
        pre = dot(u, w_in[...])
        sq = pre * pre
        th = jnp.tanh(GELU_C * pre * (1.0 + 0.044715 * sq))
        act = (0.5 * pre * (1.0 + th)).astype(b16)
        slope = 0.5 * (1.0 + th) + 0.5 * pre * (1.0 - th * th) * (GELU_C * (1.0 + 3 * 0.044715 * sq))
        hv = h[cut, :]
        d_gate = jnp.sum(act.astype(f32) * hv, axis=1, keepdims=True)
        d_pre = (gate * hv * slope).astype(b16)
        grads = pack_return(dot(d_pre, w_in[...], NT), d_gate)
        for s in range(NS):
            ret[seqs, s] = grads[s]
        ret.flush(seqs)
        act_out[cut, :] = act
        dpre_out[cut, :] = d_pre
        gate_out[cut, :] = gate


def value_body(act, w_out, out):
    out[...] = dot(act[...], w_out[...]).reshape(NE, CAP, D).astype(b16)


def unpack_return(total):
    block = total[:, :CAP].reshape(SLOTS, 128).astype(b16)
    t3 = total[:, 24:32]
    t4 = total[:, 32:40]
    return block, jnp.concatenate([t3, roll_half(t3), t4], axis=1).reshape(SLOTS, 128), t4


def collect_body(index, got, piece, d_gate):
    block, half, t4 = unpack_return(jnp.sum(got[...].astype(f32), axis=1))
    lane = lanes((SLOTS, 128))
    tl = lanes(t4.shape)
    cols = []
    for t in range(3):
        cols.append(jnp.sum(jnp.where((tl == 64 + t) | (tl == 67 + t), t4, 0.0), axis=2, keepdims=True))
    col = jnp.concatenate(cols, axis=1).reshape(SLOTS, 1)
    hi = col.astype(b16).astype(f32)
    half = jnp.where(lane < 64, half, jnp.where(lane == 64, hi, jnp.where(lane == 65, col - hi, 0.0)))
    hot = (index[...] == lanes((T, SLOTS))).astype(b16)
    mine = dot(hot, jnp.concatenate([block, half.astype(b16)], axis=1))
    piece[...] = pack_rows(mine[:, :128], mine[:, 128:])
    piece.flush()
    lt = lanes((T, 128))
    d_gate[...] = jnp.sum(jnp.where((lt == 64) | (lt == 65), mine[:, 128:], 0.0), axis=1, keepdims=True)


def backward_body(
    me, gains, d_gate, coef, router, held, hidden_in, cot, out_proj, v, p, qk_t, heads_t, u, a, bk, w,
    pay, d_proj, gain_out, dhid_out, scr, dhid,
):
    d_expert = unpack_rows([held[j] for j in range(NS)]).astype(f32)
    dg = d_gate[...]
    d_logits = coef[...] * dg
    high = d_logits.astype(b16)
    low = (d_logits - high.astype(f32)).astype(b16)
    d_u = dot(high, router[...]) + dot(low, router[...]) + d_expert
    hidden = hidden_in[...]
    r2 = inv_rms(hidden)
    n2 = hidden * r2
    gain_two = jnp.sum(d_u * n2, axis=0, keepdims=True)
    v2 = d_u * gains[1:2, :]
    d_hidden = cot[...].astype(f32) + r2 * (v2 - n2 * jnp.mean(v2 * n2, axis=-1, keepdims=True))
    dhid[...] = d_hidden
    dhid_out.flush(src=dhid.at[pl.ds(pl.multiple_of(me[0] * 128, 128), 128)])
    d_att = d_hidden.astype(b16)
    router_t = dot(high, u[...], TN) + dot(low, u[...], TN)
    g_out = dot(heads_t[...], d_att)
    do_t = dot(out_proj[...], d_att, NT).astype(b16)
    hot = bucket_hot(bk[...])
    dqs, dks, dvs, bias = [], [], [], []
    for h in range(NH):
        part = slice(HD * h, HD * h + HD)
        prob = p[h]
        dp = dot(v[:, part], do_t[part])
        delta = jnp.sum(prob * dp, axis=0, keepdims=True)
        ds = (prob * (dp - delta)).astype(b16)
        dvs.append(dot(do_t[part], prob.astype(b16), NT))
        dks.append(dot(qk_t[0, part], ds, NT) * SCALE)
        dqs.append(dot(qk_t[1, part], ds) * SCALE)
        ds_f = ds.astype(f32)
        acc = jnp.zeros((128, 1024), f32)
        for b in range(4):
            left, right = 384 - 128 * b, 128 + 128 * b
            blk = ds_f[128 * b : 128 * b + 128]
            parts = ([jnp.zeros((128, left), f32)] if left else []) + [blk, jnp.zeros((128, right), f32)]
            acc = acc + jnp.concatenate(parts, axis=1)
        for step in (64, 32, 16, 8):
            acc = acc[:step] + pltpu.roll(acc[step:], 1024 - step, 1)
        row = rows_of((8, 1024))
        for step in (4, 2, 1):
            acc = jnp.where((row & step) != 0, pltpu.roll(acc, 1024 - step, 1), acc)
        bias.append(pltpu.roll(jnp.sum(acc, axis=0, keepdims=True), 127, 1))
    bias = lax.dot_general(
        jnp.concatenate(bias + [jnp.zeros((5, 1024), f32)], axis=0), hot, NT,
        precision=lax.Precision.HIGHEST, preferred_element_type=f32,
    )
    dq = jnp.concatenate(dqs, axis=0).astype(b16)
    dk = jnp.concatenate(dks, axis=0).astype(b16)
    dv = jnp.concatenate(dvs, axis=0).astype(b16)
    for c, m in enumerate((dq, dk, dv)):
        d_proj[c] = m
    d_proj.flush()
    a_v = a[...]
    grads = [dot(m, a_v) for m in (dq, dk, dv)]
    gain_rows = [
        jnp.sum(w[c].astype(f32) * grads[c], axis=0, keepdims=True) for c in range(3)
    ]
    gain_one = gain_rows[0] + gain_rows[1] + gain_rows[2]
    full = jnp.concatenate([g.astype(b16) for g in grads + [g_out]], axis=0)
    big = jnp.concatenate([full[:, 128 * l : 128 * l + 128] for l in range(6)], axis=0)
    for c in range(NE):
        pay[c, :MAIN] = big[MAIN * c : MAIN * c + MAIN]
    scr[:, 6:, :] = jnp.zeros((NE, 10, 128), f32)
    wide = jnp.concatenate([bias, jnp.zeros((8, 96), f32)], axis=1)
    for l in range(6):
        scr[:, l, :] = router_t[:, 128 * l : 128 * l + 128]
        scr[l, 6:7, :] = gain_two[:, 128 * l : 128 * l + 128]
    for h in range(NH):
        scr[6 + h, 6:7, :] = wide[h : h + 1]
    pay[:, MAIN:, :] = scr[...].astype(b16)
    gain_out[...] = gain_one


def input_grad_body(me, gain, index, got, d_proj, w, da0, da1, da2, da3, own, grads, values):
    hot = (index[...] == lanes((T, SLOTS))).astype(b16)
    values[...] = dot(hot, got[...])
    grads[...] = dot(d_proj[0], w[0], TN) + dot(d_proj[1], w[1], TN) + dot(d_proj[2], w[2], TN)
    one = gain[...]
    hi = one.astype(b16).astype(f32)
    gl = jnp.concatenate([hi, one - hi, jnp.zeros((14, D), f32)], axis=0).astype(b16)
    own[...] = gl
    for d, out in enumerate((da0, da1, da2, da3)):
        to = pl.ds(pl.multiple_of(lax.rem(me[0] + d, NS) * 128, 128), 128)
        out[:128] = grads[to, :].astype(b16)
        out[128:144] = gl
        out[144:] = values[to, :].astype(b16)
        out.flush()


def sum_body(me, held, pay, out):
    total = jnp.sum(pay[...].astype(f32), axis=0)
    gl = jnp.sum(jnp.sum(held[...].astype(f32), axis=0), axis=0, keepdims=True)
    gl = [gl[:, 128 * l : 128 * l + 128] for l in range(6)] + [jnp.zeros((2, 128), f32)]
    chunk = jnp.concatenate([total[: MAIN + 8]] + gl, axis=0).astype(b16)
    out[...] = jnp.broadcast_to(chunk[None], (NE, PAY, 128))


def token_grad_body(me, gains, held, tok, dhid, gate, hidden, out):
    d_a = jnp.sum(held[:, :128, :].astype(f32), axis=0)
    x = tok[...].astype(f32)
    r1 = inv_rms(x)
    n1 = x * r1
    v1 = d_a * gains[0:1, :]
    grad = dhid[...] + r1 * (v1 - n1 * jnp.mean(v1 * n1, axis=-1, keepdims=True))
    value = jnp.sum(held[:, 144:, :].astype(f32), axis=0).astype(b16).astype(f32)
    out[:128] = (hidden[...] + gate[...] * value).astype(b16)
    out[128:] = grad.astype(b16)


def tokens_body(me, held, result, grad):
    held.ready()
    for j in range(NS):
        rows = pl.ds(128 * j, 128)
        result.send(held.held.at[j, pl.ds(0, 128)], rows)
        grad.send(held.held.at[j, pl.ds(128, 128)], rows)


def finish_body(got, gains, qkv, proj, bias, gains_out, router, scr):
    big = jnp.concatenate([got[c, :MAIN] for c in range(NE)], axis=0)
    full = jnp.concatenate([big[D * l : D * l + D] for l in range(6)], axis=1)
    for c in range(3):
        qkv[c] = full[W * c : W * c + W].astype(f32)
        qkv.flush(c)
    proj[...] = full[3 * W :].astype(f32)
    proj.flush()
    scr[...] = got[:, MAIN:, :].astype(f32)
    router[...] = jnp.concatenate([scr[:, l, :] for l in range(6)], axis=1)
    gl = jnp.sum(scr[:, 8:, :], axis=0)
    one = jnp.concatenate([gl[l : l + 1] for l in range(6)], axis=1) / gains[0:1, :]
    two = jnp.concatenate([scr[l, 6:7, :] for l in range(6)], axis=1)
    gains_out[...] = jnp.concatenate([one, two], axis=0)
    bias[...] = jnp.concatenate([scr[6 + h, 6:7, :NE] for h in range(NH)], axis=0)


def over_experts(v):
    return lax.all_to_all(v, "expert", split_axis=0, concat_axis=0, tiled=True)


def over_all(v):
    return lax.all_to_all(v, ("expert", "shard"), split_axis=0, concat_axis=0, tiled=True)


def rotate(v, d):
    return lax.ppermute(v, "shard", [(i, (i + d) % NS) for i in range(NS)])


def round_shard(v):
    return [v] + [rotate(v, d) for d in (1, 2, 3)]


def local(tokens, qkv_weight, out_proj, rel_bias, gains, router, w_in, w_out, route, slot, buckets, cotangent):
    w_in = w_in.reshape(D, -1)
    w_out = w_out.reshape(-1, D)
    ff = w_in.shape[1]
    me, expert = Place("shard"), Place("expert")
    route_row, slot_row = route[None, :], slot[None, :]
    bk = jnp.concatenate([jnp.flip(buckets), jnp.full((1,), -1, jnp.int32)])[None, :]
    w_t = jnp.transpose(qkv_weight, (0, 2, 1))
    router_t = router.T
    together = lax.optimization_barrier

    (g_rows,) = call(dispatch_body, [((NE, CAP, D), b16)], route_row, slot_row, cotangent, name="dispatch_cotangent")
    g_rows = over_experts(g_rows).reshape(SLOTS, D)
    w_pieces = round_shard(out_proj)
    heads, heads_t, a, qk_t, v, p = call(
        attend_body,
        [((D, 128), b16), ((W, T), b16), ((T, D), b16), ((2, W, T), b16), ((T, W), b16), ((NH, T, T), f32)],
        tokens, gains, Parts(w_t), rel_bias, bk, name="attend",
    )
    h_pieces = round_shard(heads)
    (w_full,) = call(order_weights_body, [((D, D), b16)], me, Pieces(w_pieces), name="order_weights", room=25)
    rows, u, hidden = call(
        mix_body,
        [((NE, CAP, D), b16), ((T, D), b16), ((T, D), f32)],
        me, route_row, slot_row, gains, Pieces(h_pieces), w_full, tokens, name="mix",
    )
    u_rows = over_experts(rows).reshape(SLOTS, D)
    (h,) = call(ungated_body, [((SLOTS, ff), f32)], g_rows, w_out, name="ungated")
    gate, coef, index = call(
        gate_body, [((T, 1), f32), ((T, NE), f32), ((T, 1), jnp.int32)], u, router_t, route[:, None], slot[:, None],
        name="gate",
    )
    u_rows, h, gate, coef, index = together((u_rows, h, gate, coef, index))
    ret, act, d_pre, row_gate = call(
        expert_body,
        [((NE, NS, 40, 128), b16), ((SLOTS, ff), b16), ((SLOTS, ff), b16), ((SLOTS, 1), f32)],
        expert, router_t, u_rows, w_in, h, name="expert",
    )
    back = over_all(ret.reshape(NE * NS, 40, 128)).reshape(NE, NS, 40, 128)
    (val,) = call(value_body, [((NE, CAP, D), b16)], act, w_out, name="value")
    d_rows = (row_gate * g_rows.astype(f32)).astype(b16)
    grad_w_out = dot(act, d_rows, TN)
    grad_w_in = dot(u_rows, d_pre, TN)
    back, val, grad_w_out, grad_w_in = together((back, val, grad_w_out, grad_w_in))
    piece, d_gate = call(
        collect_body, [((D, 128), b16), ((T, 1), f32)], index, back, name="collect_back", room=25
    )
    b_pieces = round_shard(piece)
    value = over_experts(val).reshape(SLOTS, D)
    pay, d_proj, gain_one, d_hidden = call(
        backward_body,
        [((NE, PAY, 128), b16), ((3, W, T), b16), ((1, D), f32), ((T // NS, D), f32)],
        me, gains, d_gate, coef, router_t, Pieces(b_pieces), hidden, cotangent, out_proj, v, Parts(p), qk_t, heads_t, u,
        a, bk, w_t, name="backward", unheld=(3,),
        scratch=[pltpu.VMEM((NE, 16, 128), f32), pltpu.VMEM((T, D), f32)],
    )
    pay, value, d_proj, gain_one = together((pay, value, d_proj, gain_one))
    pay = over_experts(pay)
    *da, own = call(
        input_grad_body, [((272, D), b16)] * NS + [((16, D), b16)], me, gain_one, index, value, d_proj, w_t, name="input_grad",
        scratch=[pltpu.VMEM((T, D), f32), pltpu.VMEM((T, D), f32)],
    )
    da = [da[0]] + [rotate(x, d) for d, x in enumerate(da) if d]
    (t_piece,) = call(
        token_grad_body, [((256, D), b16)], me, gains, Pieces(da), Quarter(tokens), d_hidden,
        Quarter(gate), Quarter(hidden), name="token_grad",
    )
    (chunk,) = call(sum_body, [((NE, PAY, 128), b16)], me, Pieces([own] + da[1:], (0, 128, 128, 128), 16), pay, name="sum_gradients", room=25)
    chunk = over_experts(chunk)
    result, grad_tokens = call(
        tokens_body, [((T, D), b16), ((T, D), b16)], me, Pieces(round_shard(t_piece)), name="tokens", room=25,
        unheld=(0, 1),
    )
    chunk, grad_tokens, result = together((chunk, grad_tokens, result))
    grad_qkv, grad_proj, grad_bias, grad_gains, grad_router = call(
        finish_body,
        [((3, W, D), f32), ((W, D), f32), ((NH, NE), f32), ((2, D), f32), ((NE, D), f32)],
        chunk, gains, name="finish", room=25, scratch=[pltpu.VMEM((NE, 16, 128), f32)],
    )
    grad_qkv = jnp.transpose(grad_qkv, (0, 2, 1))
    return (
        result, grad_tokens, grad_qkv, grad_proj, grad_bias, grad_gains, grad_router.T, grad_w_in[None],
        grad_w_out[None],
    )


def solution(mesh):
    in_specs = (
        P("expert", None),
        P(None, None, "shard"),
        P("shard", None),
        P("shard", None),
        P(),
        P(),
        P("expert", None, "shard"),
        P("expert", "shard", None),
        P("expert"),
        P("expert"),
        P(),
        P("expert", None),
    )
    out_specs = (
        P("expert", None),
        P("expert", None),
        P(None, None, "shard"),
        P("shard", None),
        P("shard", None),
        P(),
        P(),
        P("expert", None, "shard"),
        P("expert", "shard", None),
    )
    return jax.shard_map(local, mesh=mesh, in_specs=in_specs, out_specs=out_specs, check_vma=False)
```
